128 devices in a mesh: row: 4 (over y_lo, core), col: 32 (over x, y_hi, z).
Axes of the slice: x: 4, y: 4 (y_hi: 2, y_lo: 2; y = y_hi * 2 + y_lo), z: 4, core: 2. Of those that a mesh axis runs over, the one named last changes fastest.
Arguments:
- right_side: float32 [131072], P(('row', 'col')), may hold values from -6 to 6
- eigen_basis: bfloat16 [12288, 512], P(('row', 'col')), may hold values from -0.0546875 to 0.0546875
- tile_left: bfloat16 [12288, 4096], P('row', 'col'), may hold values from -0.4375 to 0.4375
- tile_right: bfloat16 [512, 12288], P('row', 'col'), may hold values from -1.25 to 1.25
- piece_owner: int32 [4, 4096], P('row', 'col'), may hold values from 0 to 131071
- omega_main: float32 [512, 512], replicated, may hold values from 0 to 1
- damping: float32 [512], replicated, may hold values from 0.05 to 1
- local_basis: bfloat16 [1024, 256, 256], P(('row', 'col')), may hold values from -0.375 to 0.375
- local_omega: float32 [1024, 256, 256], P(('row', 'col')), may hold values from 0 to 1
- local_left: bfloat16 [1024, 256, 256], P(('row', 'col')), may hold values from -0.75 to 0.75
- local_right: bfloat16 [1024, 256, 256], P(('row', 'col')), may hold values from -0.75 to 0.75
- local_owner: int32 [1024, 256], P(('row', 'col')), may hold values from 0 to 131071
Outputs:
- solution: float32 [131072], P(('row', 'col'))
- residual: float32 [131072], P(('row', 'col'))
The draws below stay inside these ranges and needn't reach their ends.
All inputs are finite; a program needn't handle non-finite values.
Results may differ from the reference program's by a relative error of at most 0.00057.
Values may be sent and summed in bfloat16 or wider, within the bound.
A program may use at most 128 MiB of HBM per device.

```python
import math
import jax
import jax.numpy as jnp
import numpy as np
from jax import lax

NORD = 12288
RANK = 512
SM = 256
SP = 256
PIECES = 128
ITERS = 2
TC = 384
MCON = 131072
LOCAL = 1024
N_ROW = 4
N_COL = 32


def place_ends(array, stream_key, low, high):
    shape = array.shape
    place = [jax.random.randint(jax.random.fold_in(stream_key, axis), (), 0, shape[axis]) for axis in range(len(shape))]
    array = array.at[tuple(place)].set(low)
    longest = shape.index(max(shape))
    place[longest] = (place[longest] + 1) % shape[longest]
    return array.at[tuple(place)].set(high)


def block_scale(key, dims, pieces, least, top_value):
    def one(position, shards_of):
        heights = jax.random.uniform(jax.random.fold_in(jax.random.fold_in(key, 6), position), (shards_of,), jnp.float32, least / len(pieces), top_value / len(pieces))
        return jnp.repeat(jnp.exp(heights), dims[position] // shards_of).reshape((-1,) + (1,) * (len(dims) - position - 1))

    loudness = one(*pieces[0])
    for cut in pieces[1:]:
        loudness = loudness * one(*cut)
    return loudness


def wide_ids(own_key, dims, count, lean):
    portions = [min(1 << octave, count + 1 - (1 << octave)) * (1 << 20) // math.isqrt((1 << octave) ** lean) + 1 for octave in range((count + 1).bit_length()) if 1 << octave <= count]
    spread = 1 + sum(portions) // (1 << 30)
    listing = np.cumsum(np.array([max(1, weight // spread) for weight in portions]))
    lot = jax.random.randint(jax.random.fold_in(own_key, 1), dims, 0, int(listing[len(portions) - 1]))
    start = jnp.left_shift(1, jnp.searchsorted(jnp.asarray(listing, jnp.int32), lot, side="right").astype(jnp.int32))
    standing = start - 1 + jax.random.randint(jax.random.fold_in(own_key, 4), dims, 0, 1 << 30) % jnp.minimum(start, count + 1 - start)
    return jax.random.permutation(jax.random.fold_in(own_key, 2), count)[standing].astype(jnp.int32)


def noise(stream_key, extent, spread, limit, split=(), kind=jnp.bfloat16):
    gain = block_scale(stream_key, extent, split, -0.22, 0.18) if split else 1.0
    result = jax.random.normal(stream_key, extent, jnp.float32) * spread * gain
    return jnp.minimum(jnp.maximum(result, -limit), limit).astype(kind)


def setup_inputs(seed: int = 0) -> dict:
    splits = jax.random.split(jax.random.key(seed), 13)
    right_side = noise(splits[0], (MCON,), 1.0, 6.0, ((0, 128),), jnp.float32)
    eigen_basis = noise(splits[1], (NORD, RANK), NORD ** -0.5, 0.0546875, ((0, 128),))
    tile_left = noise(splits[2], (NORD, N_COL * PIECES), (max(NORD // N_ROW // 16, 1)) ** -0.5, 0.4375, ((0, 4), (1, 32)))
    tile_right = noise(splits[3], (N_ROW * PIECES, N_COL * TC), (max(NORD // N_COL // 16, 1)) ** -0.5, 1.25, ((0, 4), (1, 32)))
    piece_owner = place_ends(wide_ids(splits[4], (N_ROW, N_COL * PIECES), MCON, 2), jax.random.fold_in(splits[4], 3), 0, MCON - 1).astype(jnp.int32)
    omega_main = jnp.clip(jax.random.uniform(splits[5], (RANK, RANK), jnp.float32, 0.0, 1.0), 0.0, 1.0)
    damping = jnp.clip(jax.random.uniform(splits[6], (RANK,), jnp.float32, 0.05, 1.0), 0.05, 1.0)
    local_basis = noise(splits[7], (LOCAL, SM, SM), SM ** -0.5, 0.375, ((0, 128),))
    local_omega = jnp.clip(1.0 * jax.random.uniform(splits[8], (LOCAL, SM, SM), jnp.float32) ** block_scale(splits[8], (LOCAL, SM, SM), ((0, 128),), -0.2, 0.2), 0.0, 1.0)
    local_left = noise(splits[9], (LOCAL, SP, SM), (SM // 4) ** -0.5, 0.75, ((0, 128),))
    local_right = noise(splits[10], (LOCAL, SP, SM), (SM // 4) ** -0.5, 0.75, ((0, 128),))
    local_owner = place_ends(wide_ids(splits[11], (LOCAL, SP), MCON, 1), jax.random.fold_in(splits[11], 3), 0, MCON - 1).astype(jnp.int32)
    return {"right_side": right_side, "eigen_basis": eigen_basis, "tile_left": tile_left, "tile_right": tile_right, "piece_owner": piece_owner, "omega_main": omega_main, "damping": damping, "local_basis": local_basis, "local_omega": local_omega, "local_left": local_left, "local_right": local_right, "local_owner": local_owner}


precise = lax.Precision.HIGHEST


def reference(right_side, eigen_basis, tile_left, tile_right, piece_owner, omega_main, damping, local_basis, local_omega, local_left, local_right, local_owner):
    row_len = NORD // N_ROW
    col_len = NORD // N_COL
    block_len = NORD // (N_ROW * N_COL)
    tile_count = N_ROW * N_COL
    blocked = eigen_basis.reshape(N_ROW, N_COL, block_len, RANK)
    owners = piece_owner.reshape(N_ROW, N_COL, PIECES).reshape(tile_count, PIECES)
    omega_sym = 0.5 * (omega_main + omega_main.T)
    local_sym = 0.5 * (local_omega + jnp.swapaxes(local_omega, 1, 2))
    counters = jnp.arange(tile_count, dtype=jnp.int32)
    contract = (((0,), (0,)), ((), ()))

    def fetch_tile(counter):
        tile_row = (counter // N_COL).astype(jnp.int32)
        tile_col = (counter % N_COL).astype(jnp.int32)
        left_part = lax.dynamic_slice(tile_left, (tile_row * row_len, tile_col * PIECES), (row_len, PIECES))
        right_part = lax.dynamic_slice(tile_right, (tile_row * PIECES, tile_col * col_len), (PIECES, col_len))
        return tile_row, tile_col, left_part, right_part

    def project(counter):
        tile_row, tile_col, left_part, right_part = fetch_tile(counter)
        basis_rows = lax.dynamic_slice_in_dim(eigen_basis, tile_row * row_len, row_len, 0)
        basis_cols = lax.dynamic_index_in_dim(blocked, tile_col, 1, keepdims=False).reshape(col_len, RANK)
        left_proj = lax.dot_general(left_part, basis_rows, contract, preferred_element_type=jnp.float32)
        right_proj = jnp.dot(right_part, basis_cols, preferred_element_type=jnp.float32)
        return left_proj.astype(jnp.bfloat16), right_proj.astype(jnp.bfloat16)

    left_projs, right_projs = lax.map(project, counters)
    local_lp = jnp.einsum("lps,lsk->lpk", local_left.astype(jnp.float32), local_basis.astype(jnp.float32)).astype(jnp.bfloat16)
    local_rp = jnp.einsum("lps,lsk->lpk", local_right.astype(jnp.float32), local_basis.astype(jnp.float32)).astype(jnp.bfloat16)
    left_float = local_lp.astype(jnp.float32)
    right_float = local_rp.astype(jnp.float32)

    def operate(dual_vec):
        def accumulate(field_sum, counter):
            tile_row, tile_col, left_part, right_part = fetch_tile(counter)
            coeffs = dual_vec[owners[counter]]
            scaled_right = (coeffs[:, None] * right_projs[counter].astype(jnp.float32)).astype(jnp.bfloat16)
            scaled_left = (coeffs[:, None] * left_projs[counter].astype(jnp.float32)).astype(jnp.bfloat16)
            row_terms = jnp.dot(left_part, scaled_right, preferred_element_type=jnp.float32)
            col_terms = lax.dot_general(right_part, scaled_left, contract, preferred_element_type=jnp.float32)
            field_sum = field_sum.at[tile_row].add(row_terms.reshape(N_COL, block_len, RANK))
            field_sum = field_sum.at[:, tile_col].add(col_terms.reshape(N_ROW, block_len, RANK))
            return field_sum, None

        field_sum, unused = lax.scan(accumulate, jnp.zeros((N_ROW, N_COL, block_len, RANK), jnp.float32), counters)
        field_half = field_sum.astype(jnp.bfloat16)
        curvature = lax.dot_general(eigen_basis, field_half.reshape(NORD, RANK), contract, preferred_element_type=jnp.float32)
        weights = omega_sym * curvature

        def evaluate(counter):
            tile_row, tile_col, left_part, right_part = fetch_tile(counter)
            field_rows = lax.dynamic_index_in_dim(field_half, tile_row, 0, keepdims=False).reshape(row_len, RANK)
            field_cols = lax.dynamic_index_in_dim(field_half, tile_col, 1, keepdims=False).reshape(col_len, RANK)
            left_field = lax.dot_general(left_part, field_rows, contract, preferred_element_type=jnp.float32)
            right_field = jnp.dot(right_part, field_cols, preferred_element_type=jnp.float32)
            left_proj = left_projs[counter].astype(jnp.float32)
            right_proj = right_projs[counter].astype(jnp.float32)
            left_rest = left_field - jnp.dot(left_proj, curvature, precision=precise)
            right_rest = right_field - jnp.dot(right_proj, curvature, precision=precise)
            weighted = jnp.dot(right_proj, weights, precision=precise)
            inner_sum = left_proj * weighted + left_rest * (damping * right_proj) + (damping * left_proj) * right_rest
            return 2.0 * jnp.sum(inner_sum, axis=1)

        big_values = lax.map(evaluate, counters)
        local_coeffs = dual_vec[local_owner]
        scaled = local_coeffs[:, :, None] * left_float
        half_t = jnp.einsum("lpa,lpb->lab", scaled, right_float, precision=precise)
        gram_mat = half_t + jnp.swapaxes(half_t, 1, 2)
        local_w = local_sym * gram_mat
        mixed_rows = jnp.einsum("lpb,lba->lpa", right_float, local_w, precision=precise)
        local_values = 2.0 * jnp.sum(left_float * mixed_rows, axis=2)
        totals = jnp.zeros((MCON,), jnp.float32).at[owners.reshape(-1)].add(big_values.reshape(-1))
        totals = totals.at[local_owner.reshape(-1)].add(local_values.reshape(-1))
        return dual_vec + totals

    solution = jnp.zeros_like(right_side)
    residual = right_side
    direction = right_side
    norm_now = jnp.sum(residual * residual)
    for counter in range(ITERS):
        applied = operate(direction)
        step_size = norm_now / jnp.sum(direction * applied)
        solution = solution + step_size * direction
        residual = residual - step_size * applied
        norm_next = jnp.sum(residual * residual)
        direction = residual + (norm_next / norm_now) * direction
        norm_now = norm_next
    return solution, residual
```

```python
import jax
import jax.numpy as jnp
from jax import lax
from jax.experimental import pallas as pl
from jax.experimental.pallas import tpu as pltpu
from jax.sharding import PartitionSpec as P

ITERS = 2
NR, NC = 4, 32
ND = NR * NC
MESH = pl.DeviceIdType.MESH
BF = jnp.bfloat16
F32 = jnp.float32
NN = (((1,), (0,)), ((), ()))
NT = (((1,), (1,)), ((), ()))
TN = (((0,), (0,)), ((), ()))


def dot(a, b, dims=NN):
    return lax.dot_general(a, b, dims, preferred_element_type=F32)


def pieces2(x):
    hi = x.astype(BF)
    return hi, (x - hi.astype(F32)).astype(BF)


def pieces3(x):
    hi = x.astype(BF)
    rest = x - hi.astype(F32)
    mid = rest.astype(BF)
    return hi, mid, (rest - mid.astype(F32)).astype(BF)


def place(q):
    rows = pl.ds(pl.multiple_of(lax.rem(q, 64) * 8, 8), 8)
    lanes = pl.ds(pl.multiple_of((q // 64) * 128, 128), 128)
    return rows, lanes


def spot(q):
    rows = pl.ds(pl.multiple_of((q // 4) * 16, 16), 16)
    lanes = pl.ds(pl.multiple_of(lax.rem(q, 4) * 128, 128), 128)
    return rows, lanes


def hots(owner):
    width = owner.shape[1]
    high = lax.shift_right_logical(owner, 7) & 511
    low = (lax.shift_right_logical(owner, 16) * 128) + (owner & 127)
    tall = jnp.where(lax.broadcasted_iota(jnp.int32, (512, width), 0) == high, 1.0, 0.0)
    wide = jnp.where(lax.broadcasted_iota(jnp.int32, (256, width), 0) == low, 1.0, 0.0)
    return tall.astype(BF), wide.astype(BF)


def fetch(d3, tall, wide):
    g = dot(d3, wide)
    g = g[:512] + g[512:1024] + g[1024:]
    return jnp.sum(g * tall.astype(F32), axis=0, keepdims=True)


def spread(values, tall, wide):
    x3 = jnp.concatenate(pieces3(wide.astype(F32) * values), axis=0)
    t = dot(tall, x3, NT)
    return t[:, :256] + t[:, 256:512] + t[:, 512:]


def kernel(
    rhs, p_own, u_in, v_in, own_t, own_l, omega, damp, damp_c, l_basis, l_omega, l_left, l_right,
    sol_out, res_out,
    p_rows, p_cols, u_own, v_own, vp_all, up_all, at, bt, sym, tall_l, wide_l, tall_t, wide_t,
    quad, full, vec, ret, d3, c_l, c_col, c_row, part_out, part_in, part4_out, part4_in,
    s_buf, k_out, k_in, k_red, k_full, tot, t_in, t_red, dir_own, rr_buf, ssem, rsem, lsem,
):
    i = lax.axis_index("row")
    j = lax.axis_index("col")
    me = i * NC + j
    x = j // 8
    h = lax.rem(j // 4, 2)
    z = lax.rem(j, 4)

    def line(r):
        return (i, lax.rem(j + r, NC))

    def file(r):
        return (lax.rem(i + r, NR), j)

    def dev(xx, hh, zz):
        return (i, xx * 8 + hh * 4 + zz)

    def send(src, dst, k, where):
        pltpu.make_async_remote_copy(
            src, dst, ssem.at[k], rsem.at[k], device_id=where, device_id_type=MESH
        ).start()

    def got(ref, k):
        pltpu.make_async_copy(ref, ref, rsem.at[k]).wait()

    def gone(ref, k):
        pltpu.make_async_copy(ref, ref, ssem.at[k]).wait()

    def everyone(body):
        def step(r, carry):
            o = lax.rem(me + r, ND)
            body(o, (o // NC, lax.rem(o, NC)))
            return carry

        lax.fori_loop(1, ND, step, 0)

    barrier = pltpu.get_barrier_semaphore()
    everyone(
        lambda o, where: pl.semaphore_signal(
            barrier, inc=1, device_id=where, device_id_type=MESH
        )
    )
    pl.semaphore_wait(barrier, ND - 1)

    lane_i = pl.ds(pl.multiple_of(i * 128, 128), 128)
    lane_j = pl.ds(pl.multiple_of(j * 128, 128), 128)
    for r in range(1, NR):
        o = lax.rem(i + r, NR)
        send(p_own, p_cols.at[i], 0, (o, j))
        send(v_in.at[o], v_own.at[:, lane_i], 1, (o, j))
    my_rows, my_lanes = place(me)
    everyone(lambda o, where: send(rhs, vec.at[my_rows, my_lanes], 3, where))
    half = 48
    A, B = pl.ds(0, half), pl.ds(half, half)
    send(p_own, p_rows.at[x, h, z], 4, dev(x, 1 - h, z))
    for r in (1, 3, 2):
        send(p_own.at[A], p_rows.at[x, h, z, A], 5, dev(x, h, lax.rem(z + r, 4)))
        send(p_own.at[B], p_rows.at[x, h, z, B], 5, dev(lax.rem(x + r, 4), h, z))

    p_cols[i] = p_own[...]
    p_rows[x, h, z] = p_own[...]
    v_own[:, lane_i] = v_in[i]
    vec[my_rows, my_lanes] = rhs[...]

    got(p_rows.at[0, 0, 0], 4)
    for r in (1, 3, 2):
        send(p_rows.at[x, 1 - h, z, A], p_rows.at[x, 1 - h, z, A], 5, dev(x, h, lax.rem(z + r, 4)))
        send(p_rows.at[x, 1 - h, z, B], p_rows.at[x, 1 - h, z, B], 5, dev(lax.rem(x + r, 4), h, z))

    got(p_cols.at[pl.ds(0, 3)], 0)
    vp = dot(v_in[...].reshape(384, 128), p_cols[...].reshape(384, 512), TN).astype(BF)
    vp_all[x, h, z] = vp

    tall, wide = hots(own_t[...])
    tall_t[...] = tall
    wide_t[...] = wide

    got(p_rows.at[pl.ds(0, 3), :, 0], 5)
    for r in (1, 3, 2):
        send(p_rows.at[x, :, :, A], p_rows.at[x, :, :, A], 6, dev(lax.rem(x + r, 4), h, z))
        send(p_rows.at[:, :, z, B], p_rows.at[:, :, z, B], 6, dev(x, h, lax.rem(z + r, 4)))

    def u_send(r, carry):
        o = lax.rem(j + r, NC)
        send(u_in.at[o], u_own.at[:, lane_j], 2, (i, o))
        return carry

    C, D = pl.ds(0, 64), pl.ds(64, 64)
    send(vp_all.at[x, h, z], vp_all.at[x, h, z], 7, dev(x, 1 - h, z))
    for r in (1, 3, 2):
        send(vp_all.at[x, h, z, C], vp_all.at[x, h, z, C], 8, dev(x, h, lax.rem(z + r, 4)))
        send(vp_all.at[x, h, z, D], vp_all.at[x, h, z, D], 8, dev(lax.rem(x + r, 4), h, z))
    lax.fori_loop(1, NC, u_send, 0)
    u_own[:, lane_j] = u_in[j]

    def prepare(b, carry):
        basis = l_basis[b]
        at[b] = dot(l_left[b], basis).T.astype(BF)
        bt[b] = dot(l_right[b], basis).T.astype(BF)
        om = l_omega[b]
        sym[b] = 0.5 * (om + om.T)
        tall, wide = hots(own_l[pl.ds(b, 1), :])
        tall_l[b] = tall
        wide_l[b] = wide
        return carry

    got(vp_all.at[0, 0, 0], 7)
    for r in (1, 3, 2):
        send(vp_all.at[x, 1 - h, z, C], vp_all.at[x, 1 - h, z, C], 8, dev(x, h, lax.rem(z + r, 4)))
        send(vp_all.at[x, 1 - h, z, D], vp_all.at[x, 1 - h, z, D], 8, dev(lax.rem(x + r, 4), h, z))
    lax.fori_loop(0, 4, prepare, 0)
    got(vp_all.at[pl.ds(0, 3), :, 0], 8)
    for r in (1, 3, 2):
        send(vp_all.at[x, :, :, C], vp_all.at[x, :, :, C], 9, dev(lax.rem(x + r, 4), h, z))
        send(vp_all.at[:, :, z, D], vp_all.at[:, :, z, D], 9, dev(x, h, lax.rem(z + r, 4)))

    got(p_rows.at[pl.ds(0, 3)], 6)

    def project(k, acc):
        u = u_in[pl.ds(k * 8, 8)].reshape(768, 128)
        return acc + dot(u, p_rows[k].reshape(768, 512), TN)

    up = lax.fori_loop(0, 4, project, jnp.zeros((128, 512), F32)).astype(BF)
    up_all[i] = up
    for r in range(1, NR):
        send(up_all.at[i], up_all.at[i], 10, file(r))

    lax.fori_loop(4, 8, prepare, 0)
    om = omega[...]
    quad[...] = 0.5 * (om + om.T) - damp[...] - damp_c[...]

    got(t_in.at[pl.ds(0, ND - 1)], 3)
    first = vec[...]
    ret[...] = first
    dir_own[...] = rhs[...]
    res_out[...] = rhs[...]
    sol_out[...] = jnp.zeros_like(rhs)
    rr_buf[...] = jnp.broadcast_to(jnp.sum(first * first, keepdims=True), (8, 128))

    def iterate(it, carry):
        d3[...] = jnp.concatenate(pieces3(vec[...]), axis=0)
        c_own = jnp.broadcast_to(fetch(d3[...], tall_t[...], wide_t[...]), (8, 128))
        c_col[j] = c_own
        c_row[i] = c_own

        def c_send(r, carry):
            send(c_col.at[j], c_col.at[j], 11, line(r))
            return carry

        lax.fori_loop(1, NC, c_send, 0)
        for r in range(1, NR):
            send(c_row.at[i], c_row.at[i], 12, file(r))

        def take(b, carry):
            c_l[b] = jnp.broadcast_to(fetch(d3[...], tall_l[b], wide_l[b]), (8, 256))
            return carry

        lax.fori_loop(0, 8, take, 0)

        @pl.when(it == 0)
        def _():
            got(vp_all.at[pl.ds(0, 3)], 9)
            got(u_own.at[:, pl.ds(0, 31 * 128)], 2)
            got(up_all.at[pl.ds(0, 3)], 10)
            got(v_own.at[:, pl.ds(0, 384)], 1)

        got(c_col.at[pl.ds(0, NC - 1)], 11)
        got(c_row.at[pl.ds(0, NR - 1)], 12)
        gone(c_col.at[pl.ds(0, NC - 1)], 11)
        gone(c_row.at[pl.ds(0, NR - 1)], 12)

        def add_rows(k, acc):
            lanes = pl.ds(pl.multiple_of(k * 1024, 1024), 1024)
            c = c_col[pl.ds(k * 8, 8)]
            c = jnp.concatenate([c[n, :1] for n in range(8)], axis=0).T
            v = vp_all[k].reshape(8, 128, 512)
            sv = [(v[n].astype(F32) * c[:, n : n + 1]).astype(BF) for n in range(8)]
            return acc + dot(u_own[:, lanes], jnp.concatenate(sv, axis=0))

        c = c_row[...]
        c = jnp.concatenate([c[n, :1] for n in range(NR)] * 2, axis=0).T
        su = [(up_all[n].astype(F32) * c[:, n : n + 1]).astype(BF) for n in range(NR)]
        s = lax.fori_loop(0, 4, add_rows, dot(v_own[...], jnp.concatenate(su, axis=0)))
        s = s.astype(BF)
        k_out[...] = dot(p_own[...], s, TN).astype(BF)

        def k_send(o, where):
            rows, lanes = spot(o)
            send(k_out.at[rows, lanes], k_in.at[me], 13, where)

        everyone(k_send)
        k_rows, k_lanes = spot(me)
        k_in[me] = k_out[k_rows, k_lanes]

        s_buf[...] = jnp.concatenate(pieces2(s.astype(F32) * damp[...]), axis=0)

        def field(k, carry):
            lanes = pl.ds(pl.multiple_of(k * 1024, 1024), 1024)
            t = dot(s_buf[...], vp_all[k].reshape(1024, 512), NT)
            t = (t[:96] + t[96:]) * u_own[:, lanes].astype(F32)
            t = jnp.sum(t, axis=0, keepdims=True)
            for n in range(8):
                part_out[k * 8 + n] = jnp.broadcast_to(t[:, n * 128 : (n + 1) * 128], (8, 128))
            return carry

        lax.fori_loop(0, 4, field, 0)
        t = dot(s_buf[...], up_all[...].reshape(512, 512), NT)
        t = jnp.sum((t[:96] + t[96:]) * v_own[...].astype(F32), axis=0, keepdims=True)
        for n in range(NR):
            part4_out[n] = jnp.broadcast_to(t[:, n * 128 : (n + 1) * 128], (8, 128))

        def part_send(r, carry):
            o = lax.rem(j + r, NC)
            send(part_out.at[o], part_in.at[j], 14, (i, o))
            return carry

        lax.fori_loop(1, NC, part_send, 0)
        for r in range(1, NR):
            o = lax.rem(i + r, NR)
            send(part4_out.at[o], part4_in.at[i], 15, (o, j))
        part_in[j] = part_out[j]
        part4_in[i] = part4_out[i]

        tot[...] = jnp.zeros((512, 256), F32)

        def blocks(b, carry):
            a = at[b].astype(F32)
            right = bt[b]
            hi, lo = pieces2(a * c_l[b][:1])
            half_t = dot(hi, right, NT) + dot(lo, right, NT)
            w = sym[b] * (half_t + half_t.T)
            hi, lo = pieces2(w)
            mixed = dot(hi, right) + dot(lo, right)
            values = 2.0 * jnp.sum(a * mixed, axis=0, keepdims=True)
            tot[...] += spread(values, tall_l[b], wide_l[b])
            return carry

        lax.fori_loop(0, 4, blocks, 0)

        got(k_in.at[pl.ds(0, ND - 1)], 13)
        k_red[...] = jnp.sum(k_in[...].astype(F32), axis=0).astype(BF)
        everyone(lambda o, where: send(k_red, k_full.at[k_rows, k_lanes], 16, where))
        k_full[k_rows, k_lanes] = k_red[...]
        lax.fori_loop(4, 8, blocks, 0)

        got(k_in.at[pl.ds(0, ND - 1)], 16)
        gone(k_in.at[pl.ds(0, ND - 1)], 13)
        gone(k_in.at[pl.ds(0, ND - 1)], 16)
        hi, lo = pieces2(k_full[...].astype(F32) * quad[...])
        y = dot(vp_all[x, h, z], hi) + dot(vp_all[x, h, z], lo)
        y = y * up_all[i].astype(F32)
        y = y[:, :128] + y[:, 128:256] + y[:, 256:384] + y[:, 384:]
        y = jnp.sum(y.T, axis=0, keepdims=True)
        got(part_in.at[pl.ds(0, NC - 1)], 14)
        got(part4_in.at[pl.ds(0, NR - 1)], 15)
        gone(part_in.at[pl.ds(0, NC - 1)], 14)
        gone(part4_in.at[pl.ds(0, NR - 1)], 15)
        parts = jnp.sum(part_in[...], axis=0) + jnp.sum(part4_in[...], axis=0)
        tot[...] += spread(2.0 * (y + parts[:1]), tall_t[...], wide_t[...])

        def t_send(o, where):
            rows, lanes = place(o)
            send(tot.at[rows, lanes], t_in.at[me], 17, where)

        everyone(t_send)
        t_in[me] = tot[my_rows, my_lanes]
        got(t_in.at[pl.ds(0, ND - 1)], 17)
        t_red[...] = jnp.sum(t_in[...], axis=0)
        gone(t_in.at[pl.ds(0, ND - 1)], 17)
        everyone(lambda o, where: send(t_red, full.at[my_rows, my_lanes], 18, where))
        full[my_rows, my_lanes] = t_red[...]
        got(t_in.at[pl.ds(0, ND - 1)], 18)
        gone(t_in.at[pl.ds(0, ND - 1)], 18)

        direction = vec[...]
        applied = direction + full[...]
        rr = rr_buf[...]
        step = rr / jnp.broadcast_to(jnp.sum(direction * applied, keepdims=True), (8, 128))
        sol_out[...] += step * dir_own[...]
        res_out[...] -= step * (dir_own[...] + t_red[...])
        res = ret[...] - step[:1, :1] * applied
        ret[...] = res
        new = jnp.broadcast_to(jnp.sum(res * res, keepdims=True), (8, 128))
        beta = new / rr
        vec[...] = res + beta[:1, :1] * direction
        dir_own[...] = res_out[...] + beta * dir_own[...]
        rr_buf[...] = new
        return carry

    lax.fori_loop(0, ITERS, iterate, 0)

    gone(p_cols.at[pl.ds(0, 3)], 0)
    gone(v_own.at[:, pl.ds(0, 384)], 1)
    gone(u_own.at[:, pl.ds(0, 31 * 128)], 2)
    gone(t_in.at[pl.ds(0, ND - 1)], 3)
    gone(p_rows.at[0, 0, 0], 4)
    gone(p_rows.at[pl.ds(0, 3), :, 0], 5)
    gone(p_rows.at[pl.ds(0, 3)], 6)
    gone(vp_all.at[0, 0, 0], 7)
    gone(vp_all.at[pl.ds(0, 3), :, 0], 8)
    gone(vp_all.at[pl.ds(0, 3)], 9)
    gone(up_all.at[pl.ds(0, 3)], 10)


def local(
    right_side, eigen_basis, tile_left, tile_right, piece_owner, omega_main, damping,
    local_basis, local_omega, local_left, local_right, local_owner,
):
    vmem = pl.BlockSpec(memory_space=pltpu.VMEM)
    V = pltpu.VMEM
    chunk = jax.ShapeDtypeStruct((8, 128), F32)
    scratch = [
        V((4, 2, 4, 96, 512), BF),
        V((4, 96, 512), BF),
        V((96, 4096), BF),
        V((96, 512), BF),
        V((4, 2, 4, 128, 512), BF),
        V((4, 128, 512), BF),
        V((8, 256, 256), BF),
        V((8, 256, 256), BF),
        V((8, 256, 256), F32),
        V((8, 512, 256), BF),
        V((8, 256, 256), BF),
        V((512, 128), BF),
        V((256, 128), BF),
        V((512, 512), F32),
        V((512, 256), F32),
        V((512, 256), F32),
        V((512, 256), F32),
        V((1536, 256), BF),
        V((8, 8, 256), F32),
        V((32, 8, 128), F32),
        V((4, 8, 128), F32),
        V((32, 8, 128), F32),
        V((32, 8, 128), F32),
        V((4, 8, 128), F32),
        V((4, 8, 128), F32),
        V((192, 512), BF),
        V((512, 512), BF),
        V((128, 16, 128), BF),
        V((16, 128), BF),
        V((512, 512), BF),
        V((512, 256), F32),
        V((128, 8, 128), F32),
        V((8, 128), F32),
        V((8, 128), F32),
        V((8, 128), F32),
        pltpu.SemaphoreType.DMA((19,)),
        pltpu.SemaphoreType.DMA((19,)),
        pltpu.SemaphoreType.DMA((2,)),
    ]
    out = pl.pallas_call(
        kernel,
        out_shape=(chunk, chunk),
        in_specs=[vmem] * 13,
        out_specs=(vmem, vmem),
        scratch_shapes=scratch,
        name="newton",
        compiler_params=pltpu.CompilerParams(
            collective_id=0, has_side_effects=True, vmem_limit_bytes=56 * 1024 * 1024
        ),
    )(
        right_side.reshape(8, 128),
        eigen_basis,
        tile_left.reshape(32, 96, 128),
        tile_right.T.reshape(4, 96, 128),
        piece_owner,
        local_owner,
        omega_main,
        damping.reshape(1, 512),
        damping.reshape(512, 1),
        local_basis,
        local_omega,
        local_left,
        local_right,
    )
    return out[0].reshape(-1), out[1].reshape(-1)


def solution(mesh):
    both = ("row", "col")
    placed = (
        P(both), P(both, None), P("row", "col"), P("row", "col"), P("row", "col"), P(), P(),
        P(both, None, None), P(both, None, None), P(both, None, None), P(both, None, None),
        P(both, None),
    )
    return jax.shard_map(
        local, mesh=mesh, in_specs=placed, out_specs=(P(both), P(both)), check_vma=False
    )
```

```python
import jax
import jax.numpy as jnp
from jax import lax
from jax.experimental import pallas as pl
from jax.experimental.pallas import tpu as pltpu
from jax.sharding import PartitionSpec as P

ITERS = 2
NR, NC = 4, 32
ND = NR * NC
MESH = pl.DeviceIdType.MESH
BF = jnp.bfloat16
F32 = jnp.float32
NN = (((1,), (0,)), ((), ()))
NT = (((1,), (1,)), ((), ()))
TN = (((0,), (0,)), ((), ()))


def dot(a, b, dims=NN):
    return lax.dot_general(a, b, dims, preferred_element_type=F32)


def pieces2(x):
    hi = x.astype(BF)
    return hi, (x - hi.astype(F32)).astype(BF)


def pieces3(x):
    hi = x.astype(BF)
    rest = x - hi.astype(F32)
    mid = rest.astype(BF)
    return hi, mid, (rest - mid.astype(F32)).astype(BF)


def place(q):
    rows = pl.ds(pl.multiple_of(lax.rem(q, 64) * 8, 8), 8)
    lanes = pl.ds(pl.multiple_of((q // 64) * 128, 128), 128)
    return rows, lanes


def spot(q):
    rows = pl.ds(pl.multiple_of((q // 4) * 16, 16), 16)
    lanes = pl.ds(pl.multiple_of(lax.rem(q, 4) * 128, 128), 128)
    return rows, lanes


def hots(owner):
    width = owner.shape[1]
    high = lax.shift_right_logical(owner, 7) & 511
    low = (lax.shift_right_logical(owner, 16) * 128) + (owner & 127)
    tall = jnp.where(lax.broadcasted_iota(jnp.int32, (512, width), 0) == high, 1.0, 0.0)
    wide = jnp.where(lax.broadcasted_iota(jnp.int32, (256, width), 0) == low, 1.0, 0.0)
    return tall.astype(BF), wide.astype(BF)


def fetch(d3, tall, wide):
    g = dot(d3, wide)
    g = g[:512] + g[512:1024] + g[1024:]
    return jnp.sum(g * tall.astype(F32), axis=0, keepdims=True)


def spread(values, tall, wide):
    x3 = jnp.concatenate(pieces3(wide.astype(F32) * values), axis=0)
    t = dot(tall, x3, NT)
    return t[:, :256] + t[:, 256:512] + t[:, 512:]


def kernel(
    rhs, p_own, u_in, v_raw, own_in, own_l, omega, damp, hbm_basis, hbm_omega, hbm_left, hbm_right,
    out,
    l_basis, l_omega, l_left, l_right, v_in, v_tile, u_tile, own_t,
    p_rows, p_cols, u_own, v_own, vp_all, up_all, at, bt, sym, tall_l, wide_l, tall_t, wide_t,
    quad, full, vec, ret, d3, c_l, c_col, c_row, part_out, part_in, part4_out, part4_in,
    s_buf, k_out, k_in, k_red, k_full, tot, t_in, t_red, s_out, s_in, dir_own, rr_buf,
    ssem, rsem, lsem,
):
    row = lax.axis_index("row")
    col = lax.axis_index("col")
    me = row * NC + col
    x = col // 8
    h = lax.rem(col // 4, 2)
    z = lax.rem(col, 4)
    core = lax.rem(row, 2)
    i = (row // 2) * 2 + h
    j = x * 8 + core * 4 + z
    moved = core != h
    kept = core == h

    def holder(ii, jj):
        return (
            (ii // 2) * 2 + lax.rem(jj // 4, 2),
            (jj // 8) * 8 + lax.rem(ii, 2) * 4 + lax.rem(jj, 4),
        )

    def line(r):
        return holder(i, lax.rem(j + r, NC))

    def file(r):
        return holder(lax.rem(i + r, NR), j)

    def dev(xx, zz):
        return (row, xx * 8 + h * 4 + zz)

    sibling = (row + 1 - 2 * core, col)

    def send(src, dst, k, where):
        pltpu.make_async_remote_copy(
            src, dst, ssem.at[k], rsem.at[k], device_id=where, device_id_type=MESH
        ).start()

    def got(ref, k):
        pltpu.make_async_copy(ref, ref, rsem.at[k]).wait()

    def gone(ref, k):
        pltpu.make_async_copy(ref, ref, ssem.at[k]).wait()

    def everyone(body):
        def step(r, carry):
            o = lax.rem(me + r, ND)
            body(o, (o // NC, lax.rem(o, NC)))
            return carry

        lax.fori_loop(1, ND, step, 0)

    loads = [
        pltpu.make_async_copy(src, dst, lsem.at[n])
        for n, (src, dst) in enumerate(
            [(hbm_basis, l_basis), (hbm_left, l_left), (hbm_right, l_right), (hbm_omega, l_omega)]
        )
    ]
    for load in loads:
        load.start()
    v_in[...] = v_raw[...].astype(F32).T.astype(BF).reshape(4, 96, 128)

    barrier = pltpu.get_barrier_semaphore()
    everyone(
        lambda o, where: pl.semaphore_signal(
            barrier, inc=1, device_id=where, device_id_type=MESH
        )
    )
    pl.semaphore_wait(barrier, ND - 1)

    lane_row = pl.ds(pl.multiple_of(row * 128, 128), 128)
    lane_col = pl.ds(pl.multiple_of(col * 128, 128), 128)
    for r in range(1, NR):
        o = lax.rem(row + r, NR)
        send(p_own, p_cols.at[row], 0, holder(o, col))

    @pl.when(moved)
    def _():
        send(p_own, p_cols.at[row], 19, holder(row, col))
        send(v_in, v_tile, 21, holder(row, col))
        send(own_in, own_t, 22, holder(row, col))

    @pl.when(kept)
    def _():
        p_cols[row] = p_own[...]
        v_tile[...] = v_in[...]
        own_t[...] = own_in[...]

    got(p_cols.at[pl.ds(0, 3)], 0)

    @pl.when(moved)
    def _():
        got(p_cols.at[0], 19)
        got(v_tile, 21)
        got(own_t, 22)

    A, B = pl.ds(0, 48), pl.ds(48, 48)
    for r in (1, 3, 2):
        send(p_cols.at[i, A], p_rows.at[x, core, z, A], 5, dev(x, lax.rem(z + r, 4)))
        send(p_cols.at[i, B], p_rows.at[x, core, z, B], 5, dev(lax.rem(x + r, 4), z))
    p_rows[x, core, z] = p_cols[i]

    vp = dot(v_tile[...].reshape(384, 128), p_cols[...].reshape(384, 512), TN).astype(BF)
    vp_all[x, core, z] = vp

    my_rows, my_lanes = place(me)
    everyone(lambda o, where: send(rhs, vec.at[my_rows, my_lanes], 3, where))
    vec[my_rows, my_lanes] = rhs[...]

    got(p_rows.at[pl.ds(0, 3), 0, 0], 5)
    for r in (1, 3, 2):
        send(p_rows.at[x, core, :, A], p_rows.at[x, core, :, A], 6, dev(lax.rem(x + r, 4), z))
        send(p_rows.at[:, core, z, B], p_rows.at[:, core, z, B], 6, dev(x, lax.rem(z + r, 4)))

    @pl.when(moved)
    def _():
        send(u_in, u_tile, 23, holder(row, col))

    @pl.when(kept)
    def _():
        pltpu.make_async_copy(u_in, u_tile, lsem.at[4]).start()

    C, D = pl.ds(0, 64), pl.ds(64, 64)
    for r in (1, 3, 2):
        send(vp_all.at[x, core, z, C], vp_all.at[x, core, z, C], 8, dev(x, lax.rem(z + r, 4)))
        send(vp_all.at[x, core, z, D], vp_all.at[x, core, z, D], 8, dev(lax.rem(x + r, 4), z))
    for r in range(1, NR):
        o = lax.rem(row + r, NR)
        send(v_in.at[o], v_own.at[:, lane_row], 1, holder(o, col))

    def u_send(r, carry):
        o = lax.rem(col + r, NC)
        send(u_in.at[o], u_own.at[:, lane_col], 2, holder(row, o))
        return carry

    lax.fori_loop(1, NC, u_send, 0)

    @pl.when(moved)
    def _():
        send(v_in.at[row], v_own.at[:, lane_row], 20, holder(row, col))
        send(u_in.at[col], u_own.at[:, lane_col], 24, holder(row, col))

    @pl.when(kept)
    def _():
        v_own[:, lane_row] = v_in[row]
        pltpu.make_async_copy(u_in.at[col], u_own.at[:, lane_col], lsem.at[5]).start()

    def prepare(b, carry):
        basis = l_basis[b]
        at[b] = dot(l_left[b], basis).T.astype(BF)
        bt[b] = dot(l_right[b], basis).T.astype(BF)
        om = l_omega[b]
        sym[b] = 0.5 * (om + om.T)
        tall, wide = hots(own_l[pl.ds(b, 1), :])
        tall_l[b] = tall
        wide_l[b] = wide
        return carry

    tall, wide = hots(own_t[...])
    tall_t[...] = tall
    wide_t[...] = wide
    for load in loads:
        load.wait()

    def spread_c():
        d3[...] = jnp.concatenate(pieces3(vec[...]), axis=0)
        c_own = jnp.broadcast_to(fetch(d3[...], tall_t[...], wide_t[...]), (8, 128))
        c_col[j] = c_own
        c_row[i] = c_own

        def c_send(r, carry):
            send(c_col.at[j, pl.ds(0, 1)], c_col.at[j, pl.ds(0, 1)], 11, line(r))
            return carry

        lax.fori_loop(1, NC, c_send, 0)
        for r in range(1, NR):
            send(c_row.at[i, pl.ds(0, 1)], c_row.at[i, pl.ds(0, 1)], 12, file(r))

    def take(b, carry):
        c_l[b] = jnp.broadcast_to(fetch(d3[...], tall_l[b], wide_l[b]), (8, 256))
        return carry

    lax.fori_loop(0, 2, prepare, 0)
    got(vp_all.at[pl.ds(0, 3), 0, 0], 8)
    for r in (1, 3, 2):
        send(vp_all.at[x, core, :, C], vp_all.at[x, core, :, C], 9, dev(lax.rem(x + r, 4), z))
        send(vp_all.at[:, core, z, D], vp_all.at[:, core, z, D], 9, dev(x, lax.rem(z + r, 4)))
    got(p_rows.at[:, 0, pl.ds(0, 3)], 6)
    send(p_rows.at[:, core], p_rows.at[:, core], 4, sibling)

    got(t_in.at[pl.ds(0, ND - 1)], 3)
    first = vec[...]
    ret[...] = first
    dir_own[...] = rhs[...]
    out[1] = rhs[...]
    out[0] = jnp.zeros_like(rhs)
    rr_buf[...] = jnp.broadcast_to(jnp.sum(first * first, keepdims=True), (8, 128))
    spread_c()
    lax.fori_loop(2, 5, prepare, 0)

    got(p_rows.at[:, 0], 4)

    @pl.when(moved)
    def _():
        got(u_tile, 23)

    @pl.when(kept)
    def _():
        pltpu.make_async_copy(u_in, u_tile, lsem.at[4]).wait()

    def project(k, acc):
        u = u_tile[pl.ds(k * 8, 8)].reshape(768, 128)
        return acc + dot(u, p_rows[k].reshape(768, 512), TN)

    up = lax.fori_loop(0, 4, project, jnp.zeros((128, 512), F32)).astype(BF)
    up_all[i] = up
    for r in range(1, NR):
        send(up_all.at[i], up_all.at[i], 10, file(r))

    got(vp_all.at[:, 0, pl.ds(0, 3)], 9)
    send(vp_all.at[:, core], vp_all.at[:, core], 7, sibling)
    lax.fori_loop(5, 8, prepare, 0)
    t = 0.5 * omega[...] - damp[...]
    quad[...] = t + t.T
    lax.fori_loop(0, 8, take, 0)

    got(u_own.at[:, pl.ds(0, 31 * 128)], 2)
    got(v_own.at[:, pl.ds(0, 384)], 1)

    @pl.when(moved)
    def _():
        got(v_own.at[:, pl.ds(0, 128)], 20)
        got(u_own.at[:, pl.ds(0, 128)], 24)

    @pl.when(kept)
    def _():
        pltpu.make_async_copy(u_in.at[col], u_own.at[:, lane_col], lsem.at[5]).wait()

    got(vp_all.at[:, 0], 7)
    got(up_all.at[pl.ds(0, 3)], 10)

    def iterate(it, carry):
        got(c_col.at[pl.ds(0, NC - 1), pl.ds(0, 1)], 11)
        got(c_row.at[pl.ds(0, NR - 1), pl.ds(0, 1)], 12)
        gone(c_col.at[pl.ds(0, NC - 1), pl.ds(0, 1)], 11)
        gone(c_row.at[pl.ds(0, NR - 1), pl.ds(0, 1)], 12)

        def add_rows(k, acc):
            lanes = pl.ds(pl.multiple_of(k * 1024, 1024), 1024)
            c = c_col[pl.ds(k * 8, 8)]
            c = jnp.concatenate([c[n, :1] for n in range(8)], axis=0).T
            v = vp_all[k].reshape(8, 128, 512)
            sv = [(v[n].astype(F32) * c[:, n : n + 1]).astype(BF) for n in range(8)]
            return acc + dot(u_own[:, lanes], jnp.concatenate(sv, axis=0))

        c = c_row[...]
        c = jnp.concatenate([c[n, :1] for n in range(NR)] * 2, axis=0).T
        su = [(up_all[n].astype(F32) * c[:, n : n + 1]).astype(BF) for n in range(NR)]
        s = lax.fori_loop(0, 4, add_rows, dot(v_own[...], jnp.concatenate(su, axis=0)))
        s = s.astype(BF)
        k_out[...] = dot(p_cols[i], s, TN).astype(BF)

        def k_send(o, where):
            rows, lanes = spot(o)
            send(k_out.at[rows, lanes], k_in.at[me], 13, where)

        everyone(k_send)
        k_rows, k_lanes = spot(me)
        k_in[me] = k_out[k_rows, k_lanes]

        s_buf[...] = jnp.concatenate(pieces2(s.astype(F32) * damp[...]), axis=0)

        def field(k, carry):
            lanes = pl.ds(pl.multiple_of(k * 1024, 1024), 1024)
            t = dot(s_buf[...], vp_all[k].reshape(1024, 512), NT)
            t = (t[:96] + t[96:]) * u_own[:, lanes].astype(F32)
            t = jnp.sum(t, axis=0, keepdims=True)
            for n in range(8):
                part_out[k * 8 + n] = jnp.broadcast_to(t[:, n * 128 : (n + 1) * 128], (8, 128))
            return carry

        lax.fori_loop(0, 4, field, 0)
        t = dot(s_buf[...], up_all[...].reshape(512, 512), NT)
        t = jnp.sum((t[:96] + t[96:]) * v_own[...].astype(F32), axis=0, keepdims=True)
        for n in range(NR):
            part4_out[n] = jnp.broadcast_to(t[:, n * 128 : (n + 1) * 128], (8, 128))

        def part_send(r, carry):
            o = lax.rem(j + r, NC)
            send(part_out.at[o, pl.ds(0, 1)], part_in.at[j, pl.ds(0, 1)], 14, line(r))
            return carry

        lax.fori_loop(1, NC, part_send, 0)
        for r in range(1, NR):
            o = lax.rem(i + r, NR)
            send(part4_out.at[o, pl.ds(0, 1)], part4_in.at[i, pl.ds(0, 1)], 15, file(r))
        part_in[j] = part_out[j]
        part4_in[i] = part4_out[i]

        tot[...] = jnp.zeros((512, 256), F32)

        def blocks(b, carry):
            a = at[b].astype(F32)
            right = bt[b]
            hi, lo = pieces2(a * c_l[b][:1])
            half_t = dot(hi, right, NT) + dot(lo, right, NT)
            w = sym[b] * (half_t + half_t.T)
            hi, lo = pieces2(w)
            mixed = dot(hi, right) + dot(lo, right)
            values = 2.0 * jnp.sum(a * mixed, axis=0, keepdims=True)
            tot[...] += spread(values, tall_l[b], wide_l[b])
            return carry

        lax.fori_loop(0, 4, blocks, 0)

        got(k_in.at[pl.ds(0, ND - 1)], 13)
        k_red[...] = jnp.sum(k_in[...].astype(F32), axis=0).astype(BF)
        everyone(lambda o, where: send(k_red, k_full.at[k_rows, k_lanes], 16, where))
        k_full[k_rows, k_lanes] = k_red[...]
        lax.fori_loop(4, 8, blocks, 0)

        got(k_in.at[pl.ds(0, ND - 1)], 16)
        gone(k_in.at[pl.ds(0, ND - 1)], 13)
        gone(k_in.at[pl.ds(0, ND - 1)], 16)
        hi, lo = pieces2(k_full[...].astype(F32) * quad[...])
        y = dot(vp_all[x, core, z], hi) + dot(vp_all[x, core, z], lo)
        y = y * up_all[i].astype(F32)
        y = y[:, :128] + y[:, 128:256] + y[:, 256:384] + y[:, 384:]
        y = jnp.sum(y.T, axis=0, keepdims=True)
        got(part_in.at[pl.ds(0, NC - 1), pl.ds(0, 1)], 14)
        got(part4_in.at[pl.ds(0, NR - 1), pl.ds(0, 1)], 15)
        gone(part_in.at[pl.ds(0, NC - 1), pl.ds(0, 1)], 14)
        gone(part4_in.at[pl.ds(0, NR - 1), pl.ds(0, 1)], 15)
        parts = jnp.sum(part_in[:, :1, :], axis=0) + jnp.sum(part4_in[:, :1, :], axis=0)
        tot[...] += spread(2.0 * (y + parts), tall_t[...], wide_t[...])

        def t_send(o, where):
            rows, lanes = place(o)
            send(tot.at[rows, lanes], t_in.at[me], 17, where)

        everyone(t_send)
        t_in[me] = tot[my_rows, my_lanes]
        rr = rr_buf[...]

        @pl.when(it < ITERS - 1)
        def _():
            got(t_in.at[pl.ds(0, ND - 1)], 17)
            t_red[...] = jnp.sum(t_in[...], axis=0)
            everyone(lambda o, where: send(t_red, full.at[my_rows, my_lanes], 18, where))
            full[my_rows, my_lanes] = t_red[...]
            gone(t_in.at[pl.ds(0, ND - 1)], 17)
            got(t_in.at[pl.ds(0, ND - 1)], 18)
            gone(t_in.at[pl.ds(0, ND - 1)], 18)

            direction = vec[...]
            applied = direction + full[...]
            step = rr / jnp.broadcast_to(jnp.sum(direction * applied, keepdims=True), (8, 128))
            res = ret[...] - step[:1, :1] * applied
            ret[...] = res
            new = jnp.broadcast_to(jnp.sum(res * res, keepdims=True), (8, 128))
            beta = new / rr
            vec[...] = res + beta[:1, :1] * direction
            rr_buf[...] = new
            spread_c()
            out[0] += step * dir_own[...]
            out[1] -= step * (dir_own[...] + t_red[...])
            dir_own[...] = out[1] + beta * dir_own[...]
            lax.fori_loop(0, 8, take, 0)

        @pl.when(it == ITERS - 1)
        def _():
            direction = vec[...]
            share = jnp.broadcast_to(jnp.sum(tot[...] * direction, keepdims=True), (8, 128))
            s_out[...] = share
            s_in[me] = share
            row0 = pl.ds(0, 1)
            everyone(lambda o, where: send(s_out.at[row0], s_in.at[me, row0], 18, where))
            got(t_in.at[pl.ds(0, ND - 1)], 17)
            got(s_in.at[pl.ds(0, ND - 1), row0], 18)
            whole = jnp.sum(s_in[:, :1, :], axis=0) + jnp.sum(direction * direction, keepdims=True)
            step = rr[:1] / whole
            out[0] += step * dir_own[...]
            out[1] -= step * (dir_own[...] + jnp.sum(t_in[...], axis=0))
            gone(t_in.at[pl.ds(0, ND - 1)], 17)
            gone(s_in.at[pl.ds(0, ND - 1), row0], 18)

        return carry

    lax.fori_loop(0, ITERS, iterate, 0)

    gone(p_cols.at[pl.ds(0, 3)], 0)
    gone(v_own.at[:, pl.ds(0, 384)], 1)
    gone(u_own.at[:, pl.ds(0, 31 * 128)], 2)
    gone(t_in.at[pl.ds(0, ND - 1)], 3)
    gone(p_rows.at[:, 0], 4)
    gone(p_rows.at[pl.ds(0, 3), 0, 0], 5)
    gone(p_rows.at[:, 0, pl.ds(0, 3)], 6)
    gone(vp_all.at[:, 0], 7)
    gone(vp_all.at[pl.ds(0, 3), 0, 0], 8)
    gone(vp_all.at[:, 0, pl.ds(0, 3)], 9)
    gone(up_all.at[pl.ds(0, 3)], 10)

    @pl.when(moved)
    def _():
        gone(p_cols.at[0], 19)
        gone(v_own.at[:, pl.ds(0, 128)], 20)
        gone(v_tile, 21)
        gone(own_t, 22)
        gone(u_tile, 23)
        gone(u_own.at[:, pl.ds(0, 128)], 24)


def local(
    right_side, eigen_basis, tile_left, tile_right, piece_owner, omega_main, damping,
    local_basis, local_omega, local_left, local_right, local_owner,
):
    vmem = pl.BlockSpec(memory_space=pltpu.VMEM)
    V = pltpu.VMEM
    far = pl.BlockSpec(memory_space=pl.ANY)
    scratch = [
        V((8, 256, 256), BF),
        V((8, 256, 256), F32),
        V((8, 256, 256), BF),
        V((8, 256, 256), BF),
        V((4, 96, 128), BF),
        V((4, 96, 128), BF),
        V((32, 96, 128), BF),
        V((1, 128), jnp.int32),
        V((4, 2, 4, 96, 512), BF),
        V((4, 96, 512), BF),
        V((96, 4096), BF),
        V((96, 512), BF),
        V((4, 2, 4, 128, 512), BF),
        V((4, 128, 512), BF),
        V((8, 256, 256), BF),
        V((8, 256, 256), BF),
        V((8, 256, 256), F32),
        V((8, 512, 256), BF),
        V((8, 256, 256), BF),
        V((512, 128), BF),
        V((256, 128), BF),
        V((512, 512), F32),
        V((512, 256), F32),
        V((512, 256), F32),
        V((512, 256), F32),
        V((1536, 256), BF),
        V((8, 8, 256), F32),
        V((32, 8, 128), F32),
        V((4, 8, 128), F32),
        V((32, 8, 128), F32),
        V((32, 8, 128), F32),
        V((4, 8, 128), F32),
        V((4, 8, 128), F32),
        V((192, 512), BF),
        V((512, 512), BF),
        V((128, 16, 128), BF),
        V((16, 128), BF),
        V((512, 512), BF),
        V((512, 256), F32),
        V((128, 8, 128), F32),
        V((8, 128), F32),
        V((8, 128), F32),
        V((128, 8, 128), F32),
        V((8, 128), F32),
        V((8, 128), F32),
        pltpu.SemaphoreType.DMA((25,)),
        pltpu.SemaphoreType.DMA((25,)),
        pltpu.SemaphoreType.DMA((6,)),
    ]
    out = pl.pallas_call(
        kernel,
        out_shape=jax.ShapeDtypeStruct((2, 8, 128), F32),
        in_specs=[vmem, vmem, far] + [vmem] * 5 + [far] * 4,
        out_specs=vmem,
        scratch_shapes=scratch,
        name="newton",
        compiler_params=pltpu.CompilerParams(
            collective_id=0, has_side_effects=True, vmem_limit_bytes=56 * 1024 * 1024
        ),
    )(
        right_side.reshape(8, 128),
        eigen_basis,
        tile_left.reshape(32, 96, 128),
        tile_right,
        piece_owner,
        local_owner,
        omega_main,
        damping.reshape(1, 512),
        local_basis,
        local_omega,
        local_left,
        local_right,
    )
    both = out.reshape(2, 1024)
    return both[0], both[1]


def solution(mesh):
    both = ("row", "col")
    placed = (
        P(both), P(both, None), P("row", "col"), P("row", "col"), P("row", "col"), P(), P(),
        P(both, None, None), P(both, None, None), P(both, None, None), P(both, None, None),
        P(both, None),
    )
    return jax.shard_map(
        local, mesh=mesh, in_specs=placed, out_specs=(P(both), P(both)), check_vma=False
    )
```

```python
import jax
import jax.numpy as jnp
from jax import lax
from jax.experimental import pallas as pl
from jax.experimental.pallas import tpu as pltpu
from jax.sharding import PartitionSpec as P

ITERS = 2
NR, NC = 4, 32
ND = NR * NC
MESH = pl.DeviceIdType.MESH
BF = jnp.bfloat16
F32 = jnp.float32
NN = (((1,), (0,)), ((), ()))
NT = (((1,), (1,)), ((), ()))
TN = (((0,), (0,)), ((), ()))


def dot(a, b, dims=NN):
    return lax.dot_general(a, b, dims, preferred_element_type=F32)


def pieces2(x):
    hi = x.astype(BF)
    return hi, (x - hi.astype(F32)).astype(BF)


def pieces3(x):
    hi = x.astype(BF)
    rest = x - hi.astype(F32)
    mid = rest.astype(BF)
    return hi, mid, (rest - mid.astype(F32)).astype(BF)


class Place:
    def __init__(self, x, h, z, low, core):
        self.where = (low * 2 + core, x * 8 + h * 4 + z)
        self.chunk = (
            pl.ds(pl.multiple_of(core * 256 + x * 64 + h * 32 + z * 8, 8), 8),
            pl.ds(pl.multiple_of(low * 128, 128), 128),
        )
        self.block = (
            pl.ds(pl.multiple_of(low * 256 + core * 128 + x * 32 + h * 16, 16), 16),
            pl.ds(pl.multiple_of(z * 128, 128), 128),
        )


def hots(owner):
    width = owner.shape[1]
    high = lax.shift_right_logical(owner, 7) & 511
    low = (lax.shift_right_logical(owner, 16) * 128) + (owner & 127)
    tall = jnp.where(lax.broadcasted_iota(jnp.int32, (512, width), 0) == high, 1.0, 0.0)
    wide = jnp.where(lax.broadcasted_iota(jnp.int32, (256, width), 0) == low, 1.0, 0.0)
    return tall.astype(BF), wide.astype(BF)


def fetch(d3, tall, wide):
    g = dot(d3, wide)
    g = g[:512] + g[512:1024] + g[1024:]
    return jnp.sum(g * tall.astype(F32), axis=0, keepdims=True)


def spread(values, tall, wide):
    x3 = jnp.concatenate(pieces3(wide.astype(F32) * values), axis=0)
    t = dot(tall, x3, NT)
    return t[:, :256] + t[:, 256:512] + t[:, 512:]


def kernel(
    rhs, p_own, u_in, v_raw, own_in, own_l, omega, damp, hbm_basis, hbm_omega, hbm_left, hbm_right,
    out,
    l_basis, l_omega, l_left, l_right, v_in, v_tile, u_tile, own_t,
    p_rows, p_cols, u_own, v_own, vp_all, up_all, at, bt, sym, tall_l, wide_l, tall_t, wide_t,
    quad, full, vec, ret, d3, c_l, c_me, c_col, c_row, part_out, part_in, part4_out, part4_in,
    s_buf, k_out, k_in, k_red, k_full, tot, t_in, t_red, s_out, s_in, dir_own, rr_buf,
    ssem, rsem, lsem,
):
    row = lax.axis_index("row")
    col = lax.axis_index("col")
    me = row * NC + col
    x = col // 8
    h = lax.rem(col // 4, 2)
    z = lax.rem(col, 4)
    core = lax.rem(row, 2)
    i = (row // 2) * 2 + h
    j = x * 8 + core * 4 + z
    moved = core != h
    kept = core == h

    def holder(ii, jj):
        return (
            (ii // 2) * 2 + lax.rem(jj // 4, 2),
            (jj // 8) * 8 + lax.rem(ii, 2) * 4 + lax.rem(jj, 4),
        )

    def file(r):
        return holder(lax.rem(i + r, NR), j)

    def dev(xx, zz):
        return (row, xx * 8 + h * 4 + zz)

    sibling = (row + 1 - 2 * core, col)

    def send(src, dst, k, where):
        pltpu.make_async_remote_copy(
            src, dst, ssem.at[k], rsem.at[k], device_id=where, device_id_type=MESH
        ).start()

    def got(ref, k):
        pltpu.make_async_copy(ref, ref, rsem.at[k]).wait()

    def gone(ref, k):
        pltpu.make_async_copy(ref, ref, ssem.at[k]).wait()

    ahead = (2, 3, 1, 0)
    y = h * 2 + row // 2
    zs = [lax.rem(z + k, 4) for k in ahead]
    ys = [lax.rem(y + k, 4) for k in ahead]
    ys = [(lax.rem(k, 2), k // 2) for k in ys]

    def far(k):
        return lax.rem(x + 2 + (k * (k + 1)) // 2, 4)

    def spots(count, inner, body):
        def step(k, carry):
            for at_inner in inner:
                body(k, *at_inner)
            return carry

        lax.fori_loop(0, count - 1, step, 0)
        for at_inner in inner[:-1]:
            body(count - 1, *at_inner)

    def everyone(body):
        inner = [(zz, yy) for zz in zs for yy in ys]

        def one(k, zz, yy):
            cc = lax.rem(core + 1 - k // 4, 2)
            body(Place(far(lax.rem(k, 4)), yy[1], zz, yy[0], cc))

        spots(8, inner, one)

    def plane(body):
        inner = [(cc, zz) for cc in (1 - core, core) for zz in zs]
        low = row // 2
        spots(4, inner, lambda k, cc, zz: body(far(k) * 8 + cc * 4 + zz, Place(far(k), h, zz, low, cc).where))

    loads = [
        pltpu.make_async_copy(src, dst, lsem.at[n])
        for n, (src, dst) in enumerate(
            [(hbm_basis, l_basis), (hbm_left, l_left), (hbm_right, l_right), (hbm_omega, l_omega)]
        )
    ]
    for load in loads:
        load.start()
    barrier = pltpu.get_barrier_semaphore()
    everyone(
        lambda o: pl.semaphore_signal(barrier, inc=1, device_id=o.where, device_id_type=MESH)
    )
    v_in[...] = v_raw[...].astype(F32).T.astype(BF).reshape(4, 96, 128)
    pl.semaphore_wait(barrier, ND - 1)

    lane_row = pl.ds(pl.multiple_of(row * 128, 128), 128)
    lane_col = pl.ds(pl.multiple_of(col * 128, 128), 128)

    @pl.when(moved)
    def _():
        send(p_own, p_cols.at[row], 19, holder(row, col))

    for r in range(1, NR):
        o = lax.rem(row + r, NR)
        send(p_own, p_cols.at[row], 0, holder(o, col))

    @pl.when(moved)
    def _():
        send(v_in, v_tile, 21, holder(row, col))
        send(own_in, own_t, 22, holder(row, col))

    @pl.when(kept)
    def _():
        p_cols[row] = p_own[...]
        v_tile[...] = v_in[...]
        own_t[...] = own_in[...]

    own = Place(x, h, z, row // 2, core)
    my_rows, my_lanes = own.chunk
    everyone(lambda o: send(rhs, vec.at[my_rows, my_lanes], 3, o.where))
    vec[my_rows, my_lanes] = rhs[...]

    def prepare(b, carry):
        basis = l_basis[b]
        at[b] = dot(l_left[b], basis).T.astype(BF)
        bt[b] = dot(l_right[b], basis).T.astype(BF)
        om = l_omega[b]
        sym[b] = 0.5 * (om + om.T)
        tall, wide = hots(own_l[pl.ds(b, 1), :])
        tall_l[b] = tall
        wide_l[b] = wide
        return carry

    for load in loads:
        load.wait()
    lax.fori_loop(0, 6, prepare, 0)

    @pl.when(moved)
    def _():
        got(p_cols.at[0], 19)

    A, B = pl.ds(0, 48), pl.ds(48, 48)
    for r in (1, 3, 2):
        send(p_cols.at[i, A], p_rows.at[x, core, z, A], 5, dev(x, lax.rem(z + r, 4)))
        send(p_cols.at[i, B], p_rows.at[x, core, z, B], 5, dev(lax.rem(x + r, 4), z))
    p_rows[x, core, z] = p_cols[i]

    got(p_cols.at[pl.ds(0, 3)], 0)

    @pl.when(moved)
    def _():
        got(v_tile, 21)
        got(own_t, 22)

    vp = dot(v_tile[...].reshape(384, 128), p_cols[...].reshape(384, 512), TN).astype(BF)
    vp_all[x, core, z] = vp
    C, D = pl.ds(0, 64), pl.ds(64, 64)
    for r in (1, 3, 2):
        send(vp_all.at[x, core, z, C], vp_all.at[x, core, z, C], 8, dev(x, lax.rem(z + r, 4)))
        send(vp_all.at[x, core, z, D], vp_all.at[x, core, z, D], 8, dev(lax.rem(x + r, 4), z))

    @pl.when(moved)
    def _():
        send(u_in, u_tile, 23, holder(row, col))

    @pl.when(kept)
    def _():
        pltpu.make_async_copy(u_in, u_tile, lsem.at[4]).start()

    got(p_rows.at[pl.ds(0, 3), 0, 0], 5)
    for r in (1, 3, 2):
        send(p_rows.at[x, core, :, A], p_rows.at[x, core, :, A], 6, dev(lax.rem(x + r, 4), z))
        send(p_rows.at[:, core, z, B], p_rows.at[:, core, z, B], 6, dev(x, lax.rem(z + r, 4)))

    tall, wide = hots(own_t[...])
    tall_t[...] = tall
    wide_t[...] = wide

    got(vp_all.at[pl.ds(0, 3), 0, 0], 8)
    for r in (1, 3, 2):
        send(vp_all.at[x, core, :, C], vp_all.at[x, core, :, C], 9, dev(lax.rem(x + r, 4), z))
        send(vp_all.at[:, core, z, D], vp_all.at[:, core, z, D], 9, dev(x, lax.rem(z + r, 4)))

    def u_send(k, hh, zz):
        xx = far(k)
        there = ((row // 2) * 2 + hh, xx * 8 + core * 4 + zz)
        send(u_in.at[xx * 8 + hh * 4 + zz], u_own.at[:, lane_col], 2, there)

    spots(4, [(hh, zz) for hh in (1 - h, h) for zz in zs], u_send)
    for r in range(1, NR):
        o = lax.rem(row + r, NR)
        send(v_in.at[o], v_own.at[:, lane_row], 1, holder(o, col))

    @pl.when(moved)
    def _():
        send(v_in.at[row], v_own.at[:, lane_row], 20, holder(row, col))
        send(u_in.at[col], u_own.at[:, lane_col], 24, holder(row, col))

    @pl.when(kept)
    def _():
        v_own[:, lane_row] = v_in[row]
        pltpu.make_async_copy(u_in.at[col], u_own.at[:, lane_col], lsem.at[5]).start()


    def spread_c():
        d3[...] = jnp.concatenate(pieces3(vec[...]), axis=0)
        c_own = jnp.broadcast_to(fetch(d3[...], tall_t[...], wide_t[...]), (8, 128))
        c_me[...] = c_own
        c_col[j] = c_own
        c_row[i] = c_own

        plane(lambda jj, where: send(c_me.at[pl.ds(0, 1)], c_col.at[j, pl.ds(0, 1)], 11, where))
        for r in range(1, NR):
            send(c_me.at[pl.ds(0, 1)], c_row.at[i, pl.ds(0, 1)], 12, file(r))

    def take(b, carry):
        c_l[b] = jnp.broadcast_to(fetch(d3[...], tall_l[b], wide_l[b]), (8, 256))
        return carry

    k_rows, k_lanes = own.block

    def start_k():
        c = jnp.broadcast_to(c_me[...][:1], (128, 128)).T
        c = jnp.concatenate([c] * 4, axis=1)
        vp = vp_all[x, core, z]
        up = up_all[i]
        sv = (vp.astype(F32) * c).astype(BF)
        su = (up.astype(F32) * c).astype(BF)
        k_out[...] = (dot(up, sv, TN) + dot(vp, su, TN)).astype(BF)

        def k_send(o):
            rows, lanes = o.block
            send(k_out.at[rows, lanes], k_in.at[me], 13, o.where)

        everyone(k_send)
        k_in[me] = k_out[k_rows, k_lanes]

    def turn_k():
        got(k_in.at[pl.ds(0, ND - 1)], 13)
        k_red[...] = jnp.sum(k_in[...].astype(F32), axis=0).astype(BF)
        everyone(lambda o: send(k_red, k_full.at[k_rows, k_lanes], 16, o.where))
        k_full[k_rows, k_lanes] = k_red[...]

    def blocks(b, carry):
        a = at[b].astype(F32)
        right = bt[b]
        hi, lo = pieces2(a * c_l[b][:1])
        half_t = dot(hi, right, NT) + dot(lo, right, NT)
        w = sym[b] * (half_t + half_t.T)
        hi, lo = pieces2(w)
        mixed = dot(hi, right) + dot(lo, right)
        values = 2.0 * jnp.sum(a * mixed, axis=0, keepdims=True)
        tot[...] += spread(values, tall_l[b], wide_l[b])
        return carry

    got(t_in.at[pl.ds(0, ND - 1)], 3)
    first = vec[...]
    ret[...] = first
    dir_own[...] = rhs[...]
    out[1] = rhs[...]
    out[0] = jnp.zeros_like(rhs)
    rr_buf[...] = jnp.broadcast_to(jnp.sum(first * first, keepdims=True), (8, 128))
    spread_c()
    lax.fori_loop(6, 8, prepare, 0)
    lax.fori_loop(0, 8, take, 0)
    got(p_rows.at[:, 0, pl.ds(0, 3)], 6)
    send(p_rows.at[:, core], p_rows.at[:, core], 4, sibling)

    @pl.when(moved)
    def _():
        got(u_tile, 23)

    @pl.when(kept)
    def _():
        pltpu.make_async_copy(u_in, u_tile, lsem.at[4]).wait()

    got(p_rows.at[:, 0], 4)

    def project(k, acc):
        u = u_tile[pl.ds(k * 8, 8)].reshape(768, 128)
        return acc + dot(u, p_rows[k].reshape(768, 512), TN)

    up = lax.fori_loop(0, 4, project, jnp.zeros((128, 512), F32)).astype(BF)
    up_all[i] = up
    for r in range(1, NR):
        send(up_all.at[i], up_all.at[i], 10, file(r))
    start_k()

    got(vp_all.at[:, 0, pl.ds(0, 3)], 9)
    send(vp_all.at[:, core], vp_all.at[:, core], 7, sibling)
    tot[...] = jnp.zeros((512, 256), F32)
    lax.fori_loop(0, 6, blocks, 0)
    t = 0.5 * omega[...] - damp[...]
    quad[...] = t + t.T
    turn_k()
    lax.fori_loop(6, 8, blocks, 0)

    got(u_own.at[:, pl.ds(0, 31 * 128)], 2)
    got(v_own.at[:, pl.ds(0, 384)], 1)

    @pl.when(moved)
    def _():
        got(v_own.at[:, pl.ds(0, 128)], 20)
        got(u_own.at[:, pl.ds(0, 128)], 24)

    @pl.when(kept)
    def _():
        pltpu.make_async_copy(u_in.at[col], u_own.at[:, lane_col], lsem.at[5]).wait()

    got(vp_all.at[:, 0], 7)
    got(up_all.at[pl.ds(0, 3)], 10)

    def iterate(it, carry):
        got(c_col.at[pl.ds(0, NC - 1), pl.ds(0, 1)], 11)
        got(c_row.at[pl.ds(0, NR - 1), pl.ds(0, 1)], 12)
        gone(c_col.at[pl.ds(0, NC - 1), pl.ds(0, 1)], 11)
        gone(c_row.at[pl.ds(0, NR - 1), pl.ds(0, 1)], 12)

        def add_rows(k, acc):
            lanes = pl.ds(pl.multiple_of(k * 1024, 1024), 1024)
            c = c_col[pl.ds(k * 8, 8)]
            c = jnp.concatenate([c[n, :1] for n in range(8)], axis=0).T
            v = vp_all[k].reshape(8, 128, 512)
            sv = [(v[n].astype(F32) * c[:, n : n + 1]).astype(BF) for n in range(8)]
            return acc + dot(u_own[:, lanes], jnp.concatenate(sv, axis=0))

        c = c_row[...]
        c = jnp.concatenate([c[n, :1] for n in range(NR)] * 2, axis=0).T
        su = [(up_all[n].astype(F32) * c[:, n : n + 1]).astype(BF) for n in range(NR)]
        s = lax.fori_loop(0, 4, add_rows, dot(v_own[...], jnp.concatenate(su, axis=0)))
        s = s.astype(BF)

        s_buf[...] = jnp.concatenate(pieces2(s.astype(F32) * damp[...]), axis=0)

        def field(k, carry):
            lanes = pl.ds(pl.multiple_of(k * 1024, 1024), 1024)
            t = dot(s_buf[...], vp_all[k].reshape(1024, 512), NT)
            t = (t[:96] + t[96:]) * u_own[:, lanes].astype(F32)
            t = jnp.sum(t, axis=0, keepdims=True)
            for n in range(8):
                part_out[k * 8 + n] = jnp.broadcast_to(t[:, n * 128 : (n + 1) * 128], (8, 128))
            return carry

        lax.fori_loop(0, 4, field, 0)
        t = dot(s_buf[...], up_all[...].reshape(512, 512), NT)
        t = jnp.sum((t[:96] + t[96:]) * v_own[...].astype(F32), axis=0, keepdims=True)
        for n in range(NR):
            part4_out[n] = jnp.broadcast_to(t[:, n * 128 : (n + 1) * 128], (8, 128))

        plane(
            lambda jj, where: send(
                part_out.at[jj, pl.ds(0, 1)], part_in.at[j, pl.ds(0, 1)], 14, where
            )
        )
        for r in range(1, NR):
            o = lax.rem(i + r, NR)
            send(part4_out.at[o, pl.ds(0, 1)], part4_in.at[i, pl.ds(0, 1)], 15, file(r))
        part_in[j] = part_out[j]
        part4_in[i] = part4_out[i]

        @pl.when(it > 0)
        def _():
            turn_k()
            tot[...] = jnp.zeros((512, 256), F32)
            lax.fori_loop(0, 8, blocks, 0)

        got(k_in.at[pl.ds(0, ND - 1)], 16)
        gone(k_in.at[pl.ds(0, ND - 1)], 13)
        gone(k_in.at[pl.ds(0, ND - 1)], 16)
        hi, lo = pieces2(k_full[...].astype(F32) * quad[...])
        y = dot(vp_all[x, core, z], hi) + dot(vp_all[x, core, z], lo)
        y = y * up_all[i].astype(F32)
        y = y[:, :128] + y[:, 128:256] + y[:, 256:384] + y[:, 384:]
        y = jnp.sum(y.T, axis=0, keepdims=True)
        got(part_in.at[pl.ds(0, NC - 1), pl.ds(0, 1)], 14)
        got(part4_in.at[pl.ds(0, NR - 1), pl.ds(0, 1)], 15)
        gone(part_in.at[pl.ds(0, NC - 1), pl.ds(0, 1)], 14)
        gone(part4_in.at[pl.ds(0, NR - 1), pl.ds(0, 1)], 15)
        parts = jnp.sum(part_in[:, :1, :], axis=0) + jnp.sum(part4_in[:, :1, :], axis=0)
        tot[...] += spread(2.0 * (y + parts), tall_t[...], wide_t[...])

        def t_send(o):
            rows, lanes = o.chunk
            send(tot.at[rows, lanes], t_in.at[me], 17, o.where)

        everyone(t_send)
        t_in[me] = tot[my_rows, my_lanes]
        rr = rr_buf[...]

        @pl.when(it < ITERS - 1)
        def _():
            got(t_in.at[pl.ds(0, ND - 1)], 17)
            t_red[...] = jnp.sum(t_in[...], axis=0)
            everyone(lambda o: send(t_red, full.at[my_rows, my_lanes], 18, o.where))
            full[my_rows, my_lanes] = t_red[...]
            gone(t_in.at[pl.ds(0, ND - 1)], 17)
            got(t_in.at[pl.ds(0, ND - 1)], 18)
            gone(t_in.at[pl.ds(0, ND - 1)], 18)

            direction = vec[...]
            applied = direction + full[...]
            step = rr / jnp.broadcast_to(jnp.sum(direction * applied, keepdims=True), (8, 128))
            res = ret[...] - step[:1, :1] * applied
            ret[...] = res
            new = jnp.broadcast_to(jnp.sum(res * res, keepdims=True), (8, 128))
            beta = new / rr
            vec[...] = res + beta[:1, :1] * direction
            rr_buf[...] = new
            spread_c()
            start_k()
            out[0] += step * dir_own[...]
            out[1] -= step * (dir_own[...] + t_red[...])
            dir_own[...] = out[1] + beta * dir_own[...]
            lax.fori_loop(0, 8, take, 0)

        @pl.when(it == ITERS - 1)
        def _():
            direction = vec[...]
            share = jnp.broadcast_to(jnp.sum(tot[...] * direction, keepdims=True), (8, 128))
            s_out[...] = share
            s_in[me] = share
            row0 = pl.ds(0, 1)
            everyone(lambda o: send(s_out.at[row0], s_in.at[me, row0], 18, o.where))
            got(t_in.at[pl.ds(0, ND - 1)], 17)
            got(s_in.at[pl.ds(0, ND - 1), row0], 18)
            whole = jnp.sum(s_in[:, :1, :], axis=0) + jnp.sum(direction * direction, keepdims=True)
            step = rr[:1] / whole
            out[0] += step * dir_own[...]
            out[1] -= step * (dir_own[...] + jnp.sum(t_in[...], axis=0))
            gone(t_in.at[pl.ds(0, ND - 1)], 17)
            gone(s_in.at[pl.ds(0, ND - 1), row0], 18)

        return carry

    lax.fori_loop(0, ITERS, iterate, 0)

    gone(p_cols.at[pl.ds(0, 3)], 0)
    gone(v_own.at[:, pl.ds(0, 384)], 1)
    gone(u_own.at[:, pl.ds(0, 31 * 128)], 2)
    gone(t_in.at[pl.ds(0, ND - 1)], 3)
    gone(p_rows.at[:, 0], 4)
    gone(p_rows.at[pl.ds(0, 3), 0, 0], 5)
    gone(p_rows.at[:, 0, pl.ds(0, 3)], 6)
    gone(vp_all.at[:, 0], 7)
    gone(vp_all.at[pl.ds(0, 3), 0, 0], 8)
    gone(vp_all.at[:, 0, pl.ds(0, 3)], 9)
    gone(up_all.at[pl.ds(0, 3)], 10)

    @pl.when(moved)
    def _():
        gone(p_cols.at[0], 19)
        gone(v_own.at[:, pl.ds(0, 128)], 20)
        gone(v_tile, 21)
        gone(own_t, 22)
        gone(u_tile, 23)
        gone(u_own.at[:, pl.ds(0, 128)], 24)


def local(
    right_side, eigen_basis, tile_left, tile_right, piece_owner, omega_main, damping,
    local_basis, local_omega, local_left, local_right, local_owner,
):
    vmem = pl.BlockSpec(memory_space=pltpu.VMEM)
    V = pltpu.VMEM
    far = pl.BlockSpec(memory_space=pl.ANY)
    scratch = [
        V((8, 256, 256), BF),
        V((8, 256, 256), F32),
        V((8, 256, 256), BF),
        V((8, 256, 256), BF),
        V((4, 96, 128), BF),
        V((4, 96, 128), BF),
        V((32, 96, 128), BF),
        V((1, 128), jnp.int32),
        V((4, 2, 4, 96, 512), BF),
        V((4, 96, 512), BF),
        V((96, 4096), BF),
        V((96, 512), BF),
        V((4, 2, 4, 128, 512), BF),
        V((4, 128, 512), BF),
        V((8, 256, 256), BF),
        V((8, 256, 256), BF),
        V((8, 256, 256), F32),
        V((8, 512, 256), BF),
        V((8, 256, 256), BF),
        V((512, 128), BF),
        V((256, 128), BF),
        V((512, 512), F32),
        V((512, 256), F32),
        V((512, 256), F32),
        V((512, 256), F32),
        V((1536, 256), BF),
        V((8, 8, 256), F32),
        V((8, 128), F32),
        V((32, 8, 128), F32),
        V((4, 8, 128), F32),
        V((32, 8, 128), F32),
        V((32, 8, 128), F32),
        V((4, 8, 128), F32),
        V((4, 8, 128), F32),
        V((192, 512), BF),
        V((512, 512), BF),
        V((128, 16, 128), BF),
        V((16, 128), BF),
        V((512, 512), BF),
        V((512, 256), F32),
        V((128, 8, 128), F32),
        V((8, 128), F32),
        V((8, 128), F32),
        V((128, 8, 128), F32),
        V((8, 128), F32),
        V((8, 128), F32),
        pltpu.SemaphoreType.DMA((25,)),
        pltpu.SemaphoreType.DMA((25,)),
        pltpu.SemaphoreType.DMA((6,)),
    ]
    out = pl.pallas_call(
        kernel,
        out_shape=jax.ShapeDtypeStruct((2, 8, 128), F32),
        in_specs=[vmem, vmem, far] + [vmem] * 5 + [far] * 4,
        out_specs=vmem,
        scratch_shapes=scratch,
        name="newton",
        compiler_params=pltpu.CompilerParams(
            collective_id=0, has_side_effects=True, vmem_limit_bytes=56 * 1024 * 1024
        ),
    )(
        right_side.reshape(8, 128),
        eigen_basis,
        tile_left.reshape(32, 96, 128),
        tile_right,
        piece_owner,
        local_owner,
        omega_main,
        damping.reshape(1, 512),
        local_basis,
        local_omega,
        local_left,
        local_right,
    )
    both = out.reshape(2, 1024)
    return both[0], both[1]


def solution(mesh):
    both = ("row", "col")
    placed = (
        P(both), P(both, None), P("row", "col"), P("row", "col"), P("row", "col"), P(), P(),
        P(both, None, None), P(both, None, None), P(both, None, None), P(both, None, None),
        P(both, None),
    )
    return jax.shard_map(
        local, mesh=mesh, in_specs=placed, out_specs=(P(both), P(both)), check_vma=False
    )
```

```python
import jax
import jax.numpy as jnp
from jax import lax
from jax.experimental import pallas as pl
from jax.experimental.pallas import tpu as pltpu
from jax.sharding import PartitionSpec as P

ITERS = 2
NR, NC = 4, 32
ND = NR * NC
MESH = pl.DeviceIdType.MESH
BF = jnp.bfloat16
F32 = jnp.float32
NN = (((1,), (0,)), ((), ()))
NT = (((1,), (1,)), ((), ()))
TN = (((0,), (0,)), ((), ()))


def dot(a, b, dims=NN):
    return lax.dot_general(a, b, dims, preferred_element_type=F32)


def pieces2(x):
    hi = x.astype(BF)
    return hi, (x - hi.astype(F32)).astype(BF)


def pieces3(x):
    hi = x.astype(BF)
    rest = x - hi.astype(F32)
    mid = rest.astype(BF)
    return hi, mid, (rest - mid.astype(F32)).astype(BF)


class Place:
    def __init__(self, x, h, z, low, core):
        self.where = (low * 2 + core, x * 8 + h * 4 + z)
        self.chunk = (
            pl.ds(pl.multiple_of(core * 256 + x * 64 + h * 32 + z * 8, 8), 8),
            pl.ds(pl.multiple_of(low * 128, 128), 128),
        )
        self.block = (
            pl.ds(pl.multiple_of(low * 256 + core * 128 + x * 32 + h * 16, 16), 16),
            pl.ds(pl.multiple_of(z * 128, 128), 128),
        )


def hots(owner):
    width = owner.shape[1]
    high = lax.shift_right_logical(owner, 7) & 511
    low = (lax.shift_right_logical(owner, 16) * 128) + (owner & 127)
    tall = jnp.where(lax.broadcasted_iota(jnp.int32, (512, width), 0) == high, 1.0, 0.0)
    wide = jnp.where(lax.broadcasted_iota(jnp.int32, (256, width), 0) == low, 1.0, 0.0)
    return tall.astype(BF), wide.astype(BF)


def fetch(d3, tall, wide):
    g = dot(d3, wide)
    g = g[:512] + g[512:1024] + g[1024:]
    return jnp.sum(g * tall.astype(F32), axis=0, keepdims=True)


def spread(values, tall, wide):
    x3 = jnp.concatenate(pieces3(wide.astype(F32) * values), axis=0)
    t = dot(tall, x3, NT)
    return t[:, :256] + t[:, 256:512] + t[:, 512:]


def kernel(
    rhs, p_own, u_in, v_raw, own_in, own_l, omega, damp, hbm_basis, hbm_omega, hbm_left, hbm_right,
    out,
    l_basis, l_omega, l_left, l_right, v_in, v_tile, u_tile, own_t,
    p_rows, p_cols, u_own, v_own, vp_all, up_all, at, bt, sym, tall_l, wide_l, tall_t, wide_t,
    quad, full, vec, ret, d3, c_l, c_me, c_col, c_row, part_out, part_in, part4_out, part4_in,
    s_buf, k_out, k_in, k_red, k_full, tot, t_in, t_red, s_out, s_in, dir_own, rr_buf,
    ssem, rsem, lsem,
):
    row = lax.axis_index("row")
    col = lax.axis_index("col")
    me = row * NC + col
    x = col // 8
    h = lax.rem(col // 4, 2)
    z = lax.rem(col, 4)
    core = lax.rem(row, 2)
    i = (row // 2) * 2 + h
    j = x * 8 + core * 4 + z
    moved = core != h
    kept = core == h

    def holder(ii, jj):
        return (
            (ii // 2) * 2 + lax.rem(jj // 4, 2),
            (jj // 8) * 8 + lax.rem(ii, 2) * 4 + lax.rem(jj, 4),
        )

    def file(r):
        return holder(lax.rem(i + r, NR), j)

    def dev(xx, zz):
        return (row, xx * 8 + h * 4 + zz)

    sibling = (row + 1 - 2 * core, col)

    def send(src, dst, k, where):
        pltpu.make_async_remote_copy(
            src, dst, ssem.at[k], rsem.at[k], device_id=where, device_id_type=MESH
        ).start()

    def got(ref, k):
        pltpu.make_async_copy(ref, ref, rsem.at[k]).wait()

    def gone(ref, k):
        pltpu.make_async_copy(ref, ref, ssem.at[k]).wait()

    ahead = (2, 3, 1, 0)
    y = h * 2 + row // 2
    zs = [lax.rem(z + k, 4) for k in ahead]
    ys = [lax.rem(y + k, 4) for k in ahead]
    ys = [(lax.rem(k, 2), k // 2) for k in ys]

    def far(k):
        return lax.rem(x + 2 + (k * (k + 1)) // 2, 4)

    def spots(count, inner, body):
        def step(k, carry):
            for at_inner in inner:
                body(k, *at_inner)
            return carry

        lax.fori_loop(0, count - 1, step, 0)
        for at_inner in inner[:-1]:
            body(count - 1, *at_inner)

    def everyone(body):
        inner = [(zz, yy) for zz in zs for yy in ys]

        def one(k, zz, yy):
            cc = lax.rem(core + 1 - k // 4, 2)
            body(Place(far(lax.rem(k, 4)), yy[1], zz, yy[0], cc))

        spots(8, inner, one)

    def plane(body):
        inner = [(cc, zz) for cc in (1 - core, core) for zz in zs]
        low = row // 2
        spots(4, inner, lambda k, cc, zz: body(far(k) * 8 + cc * 4 + zz, Place(far(k), h, zz, low, cc).where))

    loads = [
        pltpu.make_async_copy(src, dst, lsem.at[n])
        for n, (src, dst) in enumerate(
            [(hbm_basis, l_basis), (hbm_left, l_left), (hbm_right, l_right), (hbm_omega, l_omega)]
        )
    ]
    for load in loads:
        load.start()
    barrier = pltpu.get_barrier_semaphore()
    everyone(
        lambda o: pl.semaphore_signal(barrier, inc=1, device_id=o.where, device_id_type=MESH)
    )
    v_in[...] = v_raw[...].astype(F32).T.astype(BF).reshape(4, 96, 128)
    pl.semaphore_wait(barrier, ND - 1)

    lane_row = pl.ds(pl.multiple_of(row * 128, 128), 128)
    lane_col = pl.ds(pl.multiple_of(col * 128, 128), 128)

    @pl.when(moved)
    def _():
        send(p_own, p_cols.at[row], 19, holder(row, col))

    for r in range(1, NR):
        o = lax.rem(row + r, NR)
        send(p_own, p_cols.at[row], 0, holder(o, col))

    @pl.when(moved)
    def _():
        send(v_in, v_tile, 21, holder(row, col))
        send(own_in, own_t, 22, holder(row, col))

    @pl.when(kept)
    def _():
        p_cols[row] = p_own[...]
        v_tile[...] = v_in[...]
        own_t[...] = own_in[...]

    own = Place(x, h, z, row // 2, core)
    my_rows, my_lanes = own.chunk
    everyone(lambda o: send(rhs, vec.at[my_rows, my_lanes], 3, o.where))
    vec[my_rows, my_lanes] = rhs[...]

    def prepare(b, carry):
        basis = l_basis[b]
        at[b] = dot(l_left[b], basis).T.astype(BF)
        bt[b] = dot(l_right[b], basis).T.astype(BF)
        om = l_omega[b]
        sym[b] = 0.5 * (om + om.T)
        tall, wide = hots(own_l[pl.ds(b, 1), :])
        tall_l[b] = tall
        wide_l[b] = wide
        return carry

    for load in loads:
        load.wait()
    lax.fori_loop(0, 6, prepare, 0)
    t = 0.5 * omega[...] - damp[...]
    quad[...] = t + t.T

    @pl.when(moved)
    def _():
        got(p_cols.at[0], 19)

    A, B = pl.ds(0, 48), pl.ds(48, 48)
    for r in (1, 3, 2):
        send(p_cols.at[i, A], p_rows.at[x, core, z, A], 5, dev(x, lax.rem(z + r, 4)))
        send(p_cols.at[i, B], p_rows.at[x, core, z, B], 5, dev(lax.rem(x + r, 4), z))
    p_rows[x, core, z] = p_cols[i]

    got(p_cols.at[pl.ds(0, 3)], 0)

    @pl.when(moved)
    def _():
        got(v_tile, 21)
        got(own_t, 22)

    vp = dot(v_tile[...].reshape(384, 128), p_cols[...].reshape(384, 512), TN).astype(BF)
    vp_all[x, core, z] = vp
    C, D = pl.ds(0, 64), pl.ds(64, 64)
    for r in (1, 3, 2):
        send(vp_all.at[x, core, z, C], vp_all.at[x, core, z, C], 8, dev(x, lax.rem(z + r, 4)))
        send(vp_all.at[x, core, z, D], vp_all.at[x, core, z, D], 8, dev(lax.rem(x + r, 4), z))

    @pl.when(moved)
    def _():
        send(u_in, u_tile, 23, holder(row, col))

    @pl.when(kept)
    def _():
        pltpu.make_async_copy(u_in, u_tile, lsem.at[4]).start()

    got(p_rows.at[pl.ds(0, 3), 0, 0], 5)
    for r in (1, 3, 2):
        send(p_rows.at[x, core, :, A], p_rows.at[x, core, :, A], 6, dev(lax.rem(x + r, 4), z))
        send(p_rows.at[:, core, z, B], p_rows.at[:, core, z, B], 6, dev(x, lax.rem(z + r, 4)))

    tall, wide = hots(own_t[...])
    tall_t[...] = tall
    wide_t[...] = wide

    got(vp_all.at[pl.ds(0, 3), 0, 0], 8)
    for r in (1, 3, 2):
        send(vp_all.at[x, core, :, C], vp_all.at[x, core, :, C], 9, dev(lax.rem(x + r, 4), z))
        send(vp_all.at[:, core, z, D], vp_all.at[:, core, z, D], 9, dev(x, lax.rem(z + r, 4)))

    def u_send(k, hh, zz):
        xx = far(k)
        there = ((row // 2) * 2 + hh, xx * 8 + core * 4 + zz)
        send(u_in.at[xx * 8 + hh * 4 + zz], u_own.at[:, lane_col], 2, there)

    spots(4, [(hh, zz) for hh in (1 - h, h) for zz in zs], u_send)
    for r in range(1, NR):
        o = lax.rem(row + r, NR)
        send(v_in.at[o], v_own.at[:, lane_row], 1, holder(o, col))

    @pl.when(moved)
    def _():
        send(v_in.at[row], v_own.at[:, lane_row], 20, holder(row, col))
        send(u_in.at[col], u_own.at[:, lane_col], 24, holder(row, col))

    @pl.when(kept)
    def _():
        v_own[:, lane_row] = v_in[row]
        pltpu.make_async_copy(u_in.at[col], u_own.at[:, lane_col], lsem.at[5]).start()


    def find_c():
        d3[...] = jnp.concatenate(pieces3(vec[...]), axis=0)
        c_own = jnp.broadcast_to(fetch(d3[...], tall_t[...], wide_t[...]), (8, 128))
        c_me[...] = c_own
        c_col[j] = c_own
        c_row[i] = c_own

    def spread_c():
        plane(lambda jj, where: send(c_me.at[pl.ds(0, 1)], c_col.at[j, pl.ds(0, 1)], 11, where))
        for r in range(1, NR):
            send(c_me.at[pl.ds(0, 1)], c_row.at[i, pl.ds(0, 1)], 12, file(r))

    def take(b, carry):
        c_l[b] = jnp.broadcast_to(fetch(d3[...], tall_l[b], wide_l[b]), (8, 256))
        return carry

    k_rows, k_lanes = own.block

    def start_k():
        c = jnp.broadcast_to(c_me[...][:1], (128, 128)).T
        c = jnp.concatenate([c] * 4, axis=1)
        vp = vp_all[x, core, z]
        up = up_all[i]
        sv = (vp.astype(F32) * c).astype(BF)
        su = (up.astype(F32) * c).astype(BF)
        k_out[...] = (dot(up, sv, TN) + dot(vp, su, TN)).astype(BF)

        def k_send(o):
            rows, lanes = o.block
            send(k_out.at[rows, lanes], k_in.at[me], 13, o.where)

        everyone(k_send)
        k_in[me] = k_out[k_rows, k_lanes]

    def turn_k():
        got(k_in.at[pl.ds(0, ND - 1)], 13)
        k_red[...] = jnp.sum(k_in[...].astype(F32), axis=0).astype(BF)
        everyone(lambda o: send(k_red, k_full.at[k_rows, k_lanes], 16, o.where))
        k_full[k_rows, k_lanes] = k_red[...]

    def blocks(b, carry):
        a = at[b].astype(F32)
        right = bt[b]
        hi, lo = pieces2(a * c_l[b][:1])
        half_t = dot(hi, right, NT) + dot(lo, right, NT)
        w = sym[b] * (half_t + half_t.T)
        hi, lo = pieces2(w)
        mixed = dot(hi, right) + dot(lo, right)
        values = 2.0 * jnp.sum(a * mixed, axis=0, keepdims=True)
        tot[...] += spread(values, tall_l[b], wide_l[b])
        return carry

    got(t_in.at[pl.ds(0, ND - 1)], 3)
    first = vec[...]
    ret[...] = first
    dir_own[...] = rhs[...]
    out[1] = rhs[...]
    out[0] = jnp.zeros_like(rhs)
    rr_buf[...] = jnp.broadcast_to(jnp.sum(first * first, keepdims=True), (8, 128))
    find_c()
    spread_c()
    lax.fori_loop(6, 8, prepare, 0)
    got(p_rows.at[:, 0, pl.ds(0, 3)], 6)
    send(p_rows.at[:, core], p_rows.at[:, core], 4, sibling)
    lax.fori_loop(0, 8, take, 0)

    @pl.when(moved)
    def _():
        got(u_tile, 23)

    @pl.when(kept)
    def _():
        pltpu.make_async_copy(u_in, u_tile, lsem.at[4]).wait()

    got(p_rows.at[:, 0], 4)

    def project(k, acc):
        u = u_tile[pl.ds(k * 8, 8)].reshape(768, 128)
        return acc + dot(u, p_rows[k].reshape(768, 512), TN)

    up = lax.fori_loop(0, 4, project, jnp.zeros((128, 512), F32)).astype(BF)
    up_all[i] = up
    for r in range(1, NR):
        send(up_all.at[i], up_all.at[i], 10, file(r))
    start_k()

    got(vp_all.at[:, 0, pl.ds(0, 3)], 9)
    send(vp_all.at[:, core], vp_all.at[:, core], 7, sibling)
    tot[...] = jnp.zeros((512, 256), F32)
    lax.fori_loop(0, 8, blocks, 0)
    turn_k()

    got(u_own.at[:, pl.ds(0, 31 * 128)], 2)
    got(v_own.at[:, pl.ds(0, 384)], 1)

    @pl.when(moved)
    def _():
        got(v_own.at[:, pl.ds(0, 128)], 20)
        got(u_own.at[:, pl.ds(0, 128)], 24)

    @pl.when(kept)
    def _():
        pltpu.make_async_copy(u_in.at[col], u_own.at[:, lane_col], lsem.at[5]).wait()

    got(vp_all.at[:, 0], 7)
    got(up_all.at[pl.ds(0, 3)], 10)

    def iterate(it, carry):
        got(c_col.at[pl.ds(0, NC - 1), pl.ds(0, 1)], 11)
        got(c_row.at[pl.ds(0, NR - 1), pl.ds(0, 1)], 12)
        gone(c_col.at[pl.ds(0, NC - 1), pl.ds(0, 1)], 11)
        gone(c_row.at[pl.ds(0, NR - 1), pl.ds(0, 1)], 12)

        def add_rows(k, acc):
            lanes = pl.ds(pl.multiple_of(k * 1024, 1024), 1024)
            c = c_col[pl.ds(k * 8, 8)]
            c = jnp.concatenate([c[n, :1] for n in range(8)], axis=0).T
            v = vp_all[k].reshape(8, 128, 512)
            sv = [(v[n].astype(F32) * c[:, n : n + 1]).astype(BF) for n in range(8)]
            return acc + dot(u_own[:, lanes], jnp.concatenate(sv, axis=0))

        c = c_row[...]
        c = jnp.concatenate([c[n, :1] for n in range(NR)] * 2, axis=0).T
        su = [(up_all[n].astype(F32) * c[:, n : n + 1]).astype(BF) for n in range(NR)]
        s = lax.fori_loop(0, 4, add_rows, dot(v_own[...], jnp.concatenate(su, axis=0)))
        s = s.astype(BF)

        s_buf[...] = jnp.concatenate(pieces2(s.astype(F32) * damp[...]), axis=0)

        def field(k, carry):
            lanes = pl.ds(pl.multiple_of(k * 1024, 1024), 1024)
            t = dot(s_buf[...], vp_all[k].reshape(1024, 512), NT)
            t = (t[:96] + t[96:]) * u_own[:, lanes].astype(F32)
            t = jnp.sum(t, axis=0, keepdims=True)
            for n in range(8):
                part_out[k * 8 + n] = jnp.broadcast_to(t[:, n * 128 : (n + 1) * 128], (8, 128))
            return carry

        lax.fori_loop(0, 4, field, 0)
        t = dot(s_buf[...], up_all[...].reshape(512, 512), NT)
        t = jnp.sum((t[:96] + t[96:]) * v_own[...].astype(F32), axis=0, keepdims=True)
        for n in range(NR):
            part4_out[n] = jnp.broadcast_to(t[:, n * 128 : (n + 1) * 128], (8, 128))

        plane(
            lambda jj, where: send(
                part_out.at[jj, pl.ds(0, 1)], part_in.at[j, pl.ds(0, 1)], 14, where
            )
        )
        for r in range(1, NR):
            o = lax.rem(i + r, NR)
            send(part4_out.at[o, pl.ds(0, 1)], part4_in.at[i, pl.ds(0, 1)], 15, file(r))
        part_in[j] = part_out[j]
        part4_in[i] = part4_out[i]

        @pl.when(it > 0)
        def _():
            turn_k()
            tot[...] = jnp.zeros((512, 256), F32)
            lax.fori_loop(0, 8, blocks, 0)

        got(k_in.at[pl.ds(0, ND - 1)], 16)
        gone(k_in.at[pl.ds(0, ND - 1)], 13)
        gone(k_in.at[pl.ds(0, ND - 1)], 16)
        hi, lo = pieces2(k_full[...].astype(F32) * quad[...])
        y = dot(vp_all[x, core, z], hi) + dot(vp_all[x, core, z], lo)
        y = y * up_all[i].astype(F32)
        y = y[:, :128] + y[:, 128:256] + y[:, 256:384] + y[:, 384:]
        y = jnp.sum(y.T, axis=0, keepdims=True)
        got(part_in.at[pl.ds(0, NC - 1), pl.ds(0, 1)], 14)
        got(part4_in.at[pl.ds(0, NR - 1), pl.ds(0, 1)], 15)
        gone(part_in.at[pl.ds(0, NC - 1), pl.ds(0, 1)], 14)
        gone(part4_in.at[pl.ds(0, NR - 1), pl.ds(0, 1)], 15)
        parts = jnp.sum(part_in[:, :1, :], axis=0) + jnp.sum(part4_in[:, :1, :], axis=0)
        tot[...] += spread(2.0 * (y + parts), tall_t[...], wide_t[...])

        def t_send(o):
            rows, lanes = o.chunk
            send(tot.at[rows, lanes], t_in.at[me], 17, o.where)

        everyone(t_send)
        t_in[me] = tot[my_rows, my_lanes]
        rr = rr_buf[...]

        @pl.when(it < ITERS - 1)
        def _():
            got(t_in.at[pl.ds(0, ND - 1)], 17)
            t_red[...] = jnp.sum(t_in[...], axis=0)
            everyone(lambda o: send(t_red, full.at[my_rows, my_lanes], 18, o.where))
            full[my_rows, my_lanes] = t_red[...]
            gone(t_in.at[pl.ds(0, ND - 1)], 17)
            got(t_in.at[pl.ds(0, ND - 1)], 18)
            gone(t_in.at[pl.ds(0, ND - 1)], 18)

            direction = vec[...]
            applied = direction + full[...]
            step = rr / jnp.broadcast_to(jnp.sum(direction * applied, keepdims=True), (8, 128))
            res = ret[...] - step[:1, :1] * applied
            ret[...] = res
            new = jnp.broadcast_to(jnp.sum(res * res, keepdims=True), (8, 128))
            beta = new / rr
            vec[...] = res + beta[:1, :1] * direction
            rr_buf[...] = new
            find_c()
            start_k()
            spread_c()
            out[0] += step * dir_own[...]
            out[1] -= step * (dir_own[...] + t_red[...])
            dir_own[...] = out[1] + beta * dir_own[...]
            lax.fori_loop(0, 8, take, 0)

        @pl.when(it == ITERS - 1)
        def _():
            direction = vec[...]
            share = jnp.broadcast_to(jnp.sum(tot[...] * direction, keepdims=True), (8, 128))
            s_out[...] = share
            s_in[me] = share
            row0 = pl.ds(0, 1)
            everyone(lambda o: send(s_out.at[row0], s_in.at[me, row0], 18, o.where))
            got(t_in.at[pl.ds(0, ND - 1)], 17)
            got(s_in.at[pl.ds(0, ND - 1), row0], 18)
            whole = jnp.sum(s_in[:, :1, :], axis=0) + jnp.sum(direction * direction, keepdims=True)
            step = rr[:1] / whole
            out[0] += step * dir_own[...]
            out[1] -= step * (dir_own[...] + jnp.sum(t_in[...], axis=0))
            gone(t_in.at[pl.ds(0, ND - 1)], 17)
            gone(s_in.at[pl.ds(0, ND - 1), row0], 18)

        return carry

    lax.fori_loop(0, ITERS, iterate, 0)

    gone(p_cols.at[pl.ds(0, 3)], 0)
    gone(v_own.at[:, pl.ds(0, 384)], 1)
    gone(u_own.at[:, pl.ds(0, 31 * 128)], 2)
    gone(t_in.at[pl.ds(0, ND - 1)], 3)
    gone(p_rows.at[:, 0], 4)
    gone(p_rows.at[pl.ds(0, 3), 0, 0], 5)
    gone(p_rows.at[:, 0, pl.ds(0, 3)], 6)
    gone(vp_all.at[:, 0], 7)
    gone(vp_all.at[pl.ds(0, 3), 0, 0], 8)
    gone(vp_all.at[:, 0, pl.ds(0, 3)], 9)
    gone(up_all.at[pl.ds(0, 3)], 10)

    @pl.when(moved)
    def _():
        gone(p_cols.at[0], 19)
        gone(v_own.at[:, pl.ds(0, 128)], 20)
        gone(v_tile, 21)
        gone(own_t, 22)
        gone(u_tile, 23)
        gone(u_own.at[:, pl.ds(0, 128)], 24)


def local(
    right_side, eigen_basis, tile_left, tile_right, piece_owner, omega_main, damping,
    local_basis, local_omega, local_left, local_right, local_owner,
):
    vmem = pl.BlockSpec(memory_space=pltpu.VMEM)
    V = pltpu.VMEM
    far = pl.BlockSpec(memory_space=pl.ANY)
    scratch = [
        V((8, 256, 256), BF),
        V((8, 256, 256), F32),
        V((8, 256, 256), BF),
        V((8, 256, 256), BF),
        V((4, 96, 128), BF),
        V((4, 96, 128), BF),
        V((32, 96, 128), BF),
        V((1, 128), jnp.int32),
        V((4, 2, 4, 96, 512), BF),
        V((4, 96, 512), BF),
        V((96, 4096), BF),
        V((96, 512), BF),
        V((4, 2, 4, 128, 512), BF),
        V((4, 128, 512), BF),
        V((8, 256, 256), BF),
        V((8, 256, 256), BF),
        V((8, 256, 256), F32),
        V((8, 512, 256), BF),
        V((8, 256, 256), BF),
        V((512, 128), BF),
        V((256, 128), BF),
        V((512, 512), F32),
        V((512, 256), F32),
        V((512, 256), F32),
        V((512, 256), F32),
        V((1536, 256), BF),
        V((8, 8, 256), F32),
        V((8, 128), F32),
        V((32, 8, 128), F32),
        V((4, 8, 128), F32),
        V((32, 8, 128), F32),
        V((32, 8, 128), F32),
        V((4, 8, 128), F32),
        V((4, 8, 128), F32),
        V((192, 512), BF),
        V((512, 512), BF),
        V((128, 16, 128), BF),
        V((16, 128), BF),
        V((512, 512), BF),
        V((512, 256), F32),
        V((128, 8, 128), F32),
        V((8, 128), F32),
        V((8, 128), F32),
        V((128, 8, 128), F32),
        V((8, 128), F32),
        V((8, 128), F32),
        pltpu.SemaphoreType.DMA((25,)),
        pltpu.SemaphoreType.DMA((25,)),
        pltpu.SemaphoreType.DMA((6,)),
    ]
    out = pl.pallas_call(
        kernel,
        out_shape=jax.ShapeDtypeStruct((2, 8, 128), F32),
        in_specs=[vmem, vmem, far] + [vmem] * 5 + [far] * 4,
        out_specs=vmem,
        scratch_shapes=scratch,
        name="newton",
        compiler_params=pltpu.CompilerParams(
            collective_id=0, has_side_effects=True, vmem_limit_bytes=56 * 1024 * 1024
        ),
    )(
        right_side.reshape(8, 128),
        eigen_basis,
        tile_left.reshape(32, 96, 128),
        tile_right,
        piece_owner,
        local_owner,
        omega_main,
        damping.reshape(1, 512),
        local_basis,
        local_omega,
        local_left,
        local_right,
    )
    both = out.reshape(2, 1024)
    return both[0], both[1]


def solution(mesh):
    both = ("row", "col")
    placed = (
        P(both), P(both, None), P("row", "col"), P("row", "col"), P("row", "col"), P(), P(),
        P(both, None, None), P(both, None, None), P(both, None, None), P(both, None, None),
        P(both, None),
    )
    return jax.shard_map(
        local, mesh=mesh, in_specs=placed, out_specs=(P(both), P(both)), check_vma=False
    )
```

```python
import jax
import jax.numpy as jnp
from jax import lax
from jax.experimental import pallas as pl
from jax.experimental.pallas import tpu as pltpu
from jax.sharding import PartitionSpec as P

ITERS = 2
NR, NC = 4, 32
ND = NR * NC
MESH = pl.DeviceIdType.MESH
BF = jnp.bfloat16
F32 = jnp.float32
NN = (((1,), (0,)), ((), ()))
NT = (((1,), (1,)), ((), ()))
TN = (((0,), (0,)), ((), ()))


def dot(a, b, dims=NN):
    return lax.dot_general(a, b, dims, preferred_element_type=F32)


def pieces2(x):
    hi = x.astype(BF)
    return hi, (x - hi.astype(F32)).astype(BF)


def pieces3(x):
    hi = x.astype(BF)
    rest = x - hi.astype(F32)
    mid = rest.astype(BF)
    return hi, mid, (rest - mid.astype(F32)).astype(BF)


class Place:
    def __init__(self, x, h, z, low, core):
        self.where = (low * 2 + core, x * 8 + h * 4 + z)
        self.chunk = (
            pl.ds(pl.multiple_of(core * 256 + x * 64 + h * 32 + z * 8, 8), 8),
            pl.ds(pl.multiple_of(low * 128, 128), 128),
        )
        self.block = (
            pl.ds(pl.multiple_of(low * 256 + core * 128 + x * 32 + h * 16, 16), 16),
            pl.ds(pl.multiple_of(z * 128, 128), 128),
        )


def hots(owner):
    width = owner.shape[1]
    high = lax.shift_right_logical(owner, 7) & 511
    low = (lax.shift_right_logical(owner, 16) * 128) + (owner & 127)
    tall = jnp.where(lax.broadcasted_iota(jnp.int32, (512, width), 0) == high, 1.0, 0.0)
    wide = jnp.where(lax.broadcasted_iota(jnp.int32, (256, width), 0) == low, 1.0, 0.0)
    return tall.astype(BF), wide.astype(BF)


def fetch(d3, tall, wide):
    g = dot(d3, wide)
    g = g[:512] + g[512:1024] + g[1024:]
    return jnp.sum(g * tall.astype(F32), axis=0, keepdims=True)


def spread(values, tall, wide):
    x3 = jnp.concatenate(pieces3(wide.astype(F32) * values), axis=0)
    t = dot(tall, x3, NT)
    return t[:, :256] + t[:, 256:512] + t[:, 512:]


def kernel(
    rhs, p_own, u_in, v_raw, own_in, own_l, omega, damp, hbm_basis, hbm_omega, hbm_left, hbm_right,
    out,
    l_basis, l_omega, l_left, l_right, v_in, v_tile, u_tile, own_t,
    p_rows, p_cols, u_own, v_own, vp_all, up_all, at, bt, sym, tall_l, wide_l, tall_t, wide_t,
    quad, full, vec, ret, d3, c_l, c_me, c_col, c_row, part_out, part_in, part4_out, part4_in,
    s_buf, k_out, k_in, k_red, k_full, tot, t_in, t_red, s_out, s_in, dir_own, rr_buf,
    ssem, rsem, lsem,
):
    row = lax.axis_index("row")
    col = lax.axis_index("col")
    me = row * NC + col
    x = col // 8
    h = lax.rem(col // 4, 2)
    z = lax.rem(col, 4)
    core = lax.rem(row, 2)
    i = (row // 2) * 2 + h
    j = x * 8 + core * 4 + z
    moved = core != h
    kept = core == h

    def holder(ii, jj):
        return (
            (ii // 2) * 2 + lax.rem(jj // 4, 2),
            (jj // 8) * 8 + lax.rem(ii, 2) * 4 + lax.rem(jj, 4),
        )

    def file(r):
        return holder(lax.rem(i + r, NR), j)

    def dev(xx, zz):
        return (row, xx * 8 + h * 4 + zz)

    sibling = (row + 1 - 2 * core, col)

    def send(src, dst, k, where):
        pltpu.make_async_remote_copy(
            src, dst, ssem.at[k], rsem.at[k], device_id=where, device_id_type=MESH
        ).start()

    def got(ref, k):
        pltpu.make_async_copy(ref, ref, rsem.at[k]).wait()

    def gone(ref, k):
        pltpu.make_async_copy(ref, ref, ssem.at[k]).wait()

    ahead = (2, 3, 1, 0)
    y = h * 2 + row // 2
    zs = [lax.rem(z + k, 4) for k in ahead]
    ys = [lax.rem(y + k, 4) for k in ahead]
    ys = [(lax.rem(k, 2), k // 2) for k in ys]

    def far(k):
        return lax.rem(x + 2 + (k * (k + 1)) // 2, 4)

    def spots(count, inner, body):
        def step(k, carry):
            for at_inner in inner:
                body(k, *at_inner)
            return carry

        lax.fori_loop(0, count - 1, step, 0)
        for at_inner in inner[:-1]:
            body(count - 1, *at_inner)

    def everyone(body):
        inner = [(zz, yy) for zz in zs for yy in ys]

        def one(k, zz, yy):
            cc = lax.rem(core + 1 - k // 4, 2)
            body(Place(far(lax.rem(k, 4)), yy[1], zz, yy[0], cc))

        spots(8, inner, one)

    def plane(body):
        inner = [(cc, zz) for cc in (1 - core, core) for zz in zs]
        low = row // 2
        spots(4, inner, lambda k, cc, zz: body(far(k) * 8 + cc * 4 + zz, Place(far(k), h, zz, low, cc).where))

    loads = [
        pltpu.make_async_copy(src, dst, lsem.at[n])
        for n, (src, dst) in enumerate(
            [(hbm_basis, l_basis), (hbm_left, l_left), (hbm_right, l_right), (hbm_omega, l_omega)]
        )
    ]
    for load in loads:
        load.start()
    barrier = pltpu.get_barrier_semaphore()
    everyone(
        lambda o: pl.semaphore_signal(barrier, inc=1, device_id=o.where, device_id_type=MESH)
    )
    v_in[...] = v_raw[...].astype(F32).T.astype(BF).reshape(4, 96, 128)
    pl.semaphore_wait(barrier, ND - 1)

    lane_row = pl.ds(pl.multiple_of(row * 128, 128), 128)
    lane_col = pl.ds(pl.multiple_of(col * 128, 128), 128)

    @pl.when(moved)
    def _():
        send(p_own, p_cols.at[row], 19, holder(row, col))

    for r in range(1, NR):
        o = lax.rem(row + r, NR)
        send(p_own, p_cols.at[row], 0, holder(o, col))

    @pl.when(moved)
    def _():
        send(v_in, v_tile, 21, holder(row, col))
        send(own_in, own_t, 22, holder(row, col))

    @pl.when(kept)
    def _():
        p_cols[row] = p_own[...]
        v_tile[...] = v_in[...]
        own_t[...] = own_in[...]

    own = Place(x, h, z, row // 2, core)
    my_rows, my_lanes = own.chunk
    everyone(lambda o: send(rhs, vec.at[my_rows, my_lanes], 3, o.where))
    vec[my_rows, my_lanes] = rhs[...]

    def prepare(b, carry):
        basis = l_basis[b]
        at[b] = dot(l_left[b], basis).T.astype(BF)
        bt[b] = dot(l_right[b], basis).T.astype(BF)
        om = l_omega[b]
        sym[b] = 0.5 * (om + om.T)
        tall, wide = hots(own_l[pl.ds(b, 1), :])
        tall_l[b] = tall
        wide_l[b] = wide
        return carry

    for load in loads:
        load.wait()
    lax.fori_loop(0, 6, prepare, 0)
    t = 0.5 * omega[...] - damp[...]
    quad[...] = t + t.T

    @pl.when(moved)
    def _():
        got(p_cols.at[0], 19)

    A, B = pl.ds(0, 48), pl.ds(48, 48)
    for r in (1, 3, 2):
        send(p_cols.at[i, A], p_rows.at[x, core, z, A], 5, dev(x, lax.rem(z + r, 4)))
        send(p_cols.at[i, B], p_rows.at[x, core, z, B], 5, dev(lax.rem(x + r, 4), z))
    p_rows[x, core, z] = p_cols[i]

    got(p_cols.at[pl.ds(0, 3)], 0)

    @pl.when(moved)
    def _():
        got(v_tile, 21)
        got(own_t, 22)

    vp = dot(v_tile[...].reshape(384, 128), p_cols[...].reshape(384, 512), TN).astype(BF)
    vp_all[x, core, z] = vp
    C, D = pl.ds(0, 64), pl.ds(64, 64)
    for r in (1, 3, 2):
        send(vp_all.at[x, core, z, C], vp_all.at[x, core, z, C], 8, dev(x, lax.rem(z + r, 4)))
        send(vp_all.at[x, core, z, D], vp_all.at[x, core, z, D], 8, dev(lax.rem(x + r, 4), z))

    @pl.when(moved)
    def _():
        send(u_in, u_tile, 23, holder(row, col))

    @pl.when(kept)
    def _():
        pltpu.make_async_copy(u_in, u_tile, lsem.at[4]).start()

    got(p_rows.at[pl.ds(0, 3), 0, 0], 5)
    for r in (1, 3, 2):
        send(p_rows.at[x, core, :, A], p_rows.at[x, core, :, A], 6, dev(lax.rem(x + r, 4), z))
        send(p_rows.at[:, core, z, B], p_rows.at[:, core, z, B], 6, dev(x, lax.rem(z + r, 4)))

    tall, wide = hots(own_t[...])
    tall_t[...] = tall
    wide_t[...] = wide

    got(vp_all.at[pl.ds(0, 3), 0, 0], 8)
    for r in (1, 3, 2):
        send(vp_all.at[x, core, :, C], vp_all.at[x, core, :, C], 9, dev(lax.rem(x + r, 4), z))
        send(vp_all.at[:, core, z, D], vp_all.at[:, core, z, D], 9, dev(x, lax.rem(z + r, 4)))

    def u_send(k, hh, zz):
        xx = far(k)
        there = ((row // 2) * 2 + hh, xx * 8 + core * 4 + zz)
        send(u_in.at[xx * 8 + hh * 4 + zz], u_own.at[:, lane_col], 2, there)

    spots(4, [(hh, zz) for hh in (1 - h, h) for zz in zs], u_send)
    for r in range(1, NR):
        o = lax.rem(row + r, NR)
        send(v_in.at[o], v_own.at[:, lane_row], 1, holder(o, col))

    @pl.when(moved)
    def _():
        send(v_in.at[row], v_own.at[:, lane_row], 20, holder(row, col))
        send(u_in.at[col], u_own.at[:, lane_col], 24, holder(row, col))

    @pl.when(kept)
    def _():
        v_own[:, lane_row] = v_in[row]
        pltpu.make_async_copy(u_in.at[col], u_own.at[:, lane_col], lsem.at[5]).start()


    def spread_c():
        d3[...] = jnp.concatenate(pieces3(vec[...]), axis=0)
        c_own = jnp.broadcast_to(fetch(d3[...], tall_t[...], wide_t[...]), (8, 128))
        c_me[...] = c_own
        c_col[j] = c_own
        c_row[i] = c_own

        plane(lambda jj, where: send(c_me.at[pl.ds(0, 1)], c_col.at[j, pl.ds(0, 1)], 11, where))
        for r in range(1, NR):
            send(c_me.at[pl.ds(0, 1)], c_row.at[i, pl.ds(0, 1)], 12, file(r))

    def take(b, carry):
        c_l[b] = jnp.broadcast_to(fetch(d3[...], tall_l[b], wide_l[b]), (8, 256))
        return carry

    k_rows, k_lanes = own.block

    def start_k():
        c = jnp.broadcast_to(c_me[...][:1], (128, 128)).T
        c = jnp.concatenate([c] * 4, axis=1)
        vp = vp_all[x, core, z]
        up = up_all[i]
        sv = (vp.astype(F32) * c).astype(BF)
        su = (up.astype(F32) * c).astype(BF)
        k_out[...] = (dot(up, sv, TN) + dot(vp, su, TN)).astype(BF)

        def k_send(o):
            rows, lanes = o.block
            send(k_out.at[rows, lanes], k_in.at[me], 13, o.where)

        everyone(k_send)
        k_in[me] = k_out[k_rows, k_lanes]

    def turn_k():
        got(k_in.at[pl.ds(0, ND - 1)], 13)
        k_red[...] = jnp.sum(k_in[...].astype(F32), axis=0).astype(BF)
        everyone(lambda o: send(k_red, k_full.at[k_rows, k_lanes], 16, o.where))
        k_full[k_rows, k_lanes] = k_red[...]

    def blocks(b, carry):
        a = at[b].astype(F32)
        right = bt[b]
        hi, lo = pieces2(a * c_l[b][:1])
        half_t = dot(hi, right, NT) + dot(lo, right, NT)
        w = sym[b] * (half_t + half_t.T)
        hi, lo = pieces2(w)
        mixed = dot(hi, right) + dot(lo, right)
        values = 2.0 * jnp.sum(a * mixed, axis=0, keepdims=True)
        tot[...] += spread(values, tall_l[b], wide_l[b])
        return carry

    got(t_in.at[pl.ds(0, ND - 1)], 3)
    first = vec[...]
    ret[...] = first
    dir_own[...] = rhs[...]
    out[1] = rhs[...]
    out[0] = jnp.zeros_like(rhs)
    rr_buf[...] = jnp.broadcast_to(jnp.sum(first * first, keepdims=True), (8, 128))
    spread_c()
    lax.fori_loop(6, 8, prepare, 0)
    got(p_rows.at[:, 0, pl.ds(0, 3)], 6)
    send(p_rows.at[:, core], p_rows.at[:, core], 4, sibling)
    lax.fori_loop(0, 8, take, 0)

    @pl.when(moved)
    def _():
        got(u_tile, 23)

    @pl.when(kept)
    def _():
        pltpu.make_async_copy(u_in, u_tile, lsem.at[4]).wait()

    got(p_rows.at[:, 0], 4)

    def project(k, acc):
        u = u_tile[pl.ds(k * 8, 8)].reshape(768, 128)
        return acc + dot(u, p_rows[k].reshape(768, 512), TN)

    up = lax.fori_loop(0, 4, project, jnp.zeros((128, 512), F32)).astype(BF)
    up_all[i] = up
    for r in range(1, NR):
        send(up_all.at[i], up_all.at[i], 10, file(r))
    start_k()

    got(vp_all.at[:, 0, pl.ds(0, 3)], 9)
    send(vp_all.at[:, core], vp_all.at[:, core], 7, sibling)
    tot[...] = jnp.zeros((512, 256), F32)
    lax.fori_loop(0, 8, blocks, 0)
    turn_k()

    got(u_own.at[:, pl.ds(0, 31 * 128)], 2)
    got(v_own.at[:, pl.ds(0, 384)], 1)

    @pl.when(moved)
    def _():
        got(v_own.at[:, pl.ds(0, 128)], 20)
        got(u_own.at[:, pl.ds(0, 128)], 24)

    @pl.when(kept)
    def _():
        pltpu.make_async_copy(u_in.at[col], u_own.at[:, lane_col], lsem.at[5]).wait()

    got(vp_all.at[:, 0], 7)
    got(up_all.at[pl.ds(0, 3)], 10)

    def iterate(it, carry):
        got(c_col.at[pl.ds(0, NC - 1), pl.ds(0, 1)], 11)
        got(c_row.at[pl.ds(0, NR - 1), pl.ds(0, 1)], 12)
        gone(c_col.at[pl.ds(0, NC - 1), pl.ds(0, 1)], 11)
        gone(c_row.at[pl.ds(0, NR - 1), pl.ds(0, 1)], 12)

        def add_rows(k, acc):
            lanes = pl.ds(pl.multiple_of(k * 1024, 1024), 1024)
            c = c_col[pl.ds(k * 8, 8)]
            c = jnp.concatenate([c[n, :1] for n in range(8)], axis=0).T
            v = vp_all[k].reshape(8, 128, 512)
            sv = [(v[n].astype(F32) * c[:, n : n + 1]).astype(BF) for n in range(8)]
            return acc + dot(u_own[:, lanes], jnp.concatenate(sv, axis=0))

        c = c_row[...]
        c = jnp.concatenate([c[n, :1] for n in range(NR)] * 2, axis=0).T
        su = [(up_all[n].astype(F32) * c[:, n : n + 1]).astype(BF) for n in range(NR)]
        s = lax.fori_loop(0, 4, add_rows, dot(v_own[...], jnp.concatenate(su, axis=0)))
        s = s.astype(BF)

        s_buf[...] = jnp.concatenate(pieces2(s.astype(F32) * damp[...]), axis=0)

        def field(k, carry):
            lanes = pl.ds(pl.multiple_of(k * 1024, 1024), 1024)
            t = dot(s_buf[...], vp_all[k].reshape(1024, 512), NT)
            t = (t[:96] + t[96:]) * u_own[:, lanes].astype(F32)
            t = jnp.sum(t, axis=0, keepdims=True)
            for n in range(8):
                part_out[k * 8 + n] = jnp.broadcast_to(t[:, n * 128 : (n + 1) * 128], (8, 128))
            return carry

        lax.fori_loop(0, 4, field, 0)
        t = dot(s_buf[...], up_all[...].reshape(512, 512), NT)
        t = jnp.sum((t[:96] + t[96:]) * v_own[...].astype(F32), axis=0, keepdims=True)
        for n in range(NR):
            part4_out[n] = jnp.broadcast_to(t[:, n * 128 : (n + 1) * 128], (8, 128))

        plane(
            lambda jj, where: send(
                part_out.at[jj, pl.ds(0, 1)], part_in.at[j, pl.ds(0, 1)], 14, where
            )
        )
        for r in range(1, NR):
            o = lax.rem(i + r, NR)
            send(part4_out.at[o, pl.ds(0, 1)], part4_in.at[i, pl.ds(0, 1)], 15, file(r))
        part_in[j] = part_out[j]
        part4_in[i] = part4_out[i]

        @pl.when(it > 0)
        def _():
            turn_k()
            lax.fori_loop(0, 8, take, 0)
            tot[...] = jnp.zeros((512, 256), F32)
            lax.fori_loop(0, 8, blocks, 0)

        got(k_in.at[pl.ds(0, ND - 1)], 16)
        gone(k_in.at[pl.ds(0, ND - 1)], 13)
        gone(k_in.at[pl.ds(0, ND - 1)], 16)
        hi, lo = pieces2(k_full[...].astype(F32) * quad[...])
        y = dot(vp_all[x, core, z], hi) + dot(vp_all[x, core, z], lo)
        y = y * up_all[i].astype(F32)
        y = y[:, :128] + y[:, 128:256] + y[:, 256:384] + y[:, 384:]
        y = jnp.sum(y.T, axis=0, keepdims=True)
        got(part_in.at[pl.ds(0, NC - 1), pl.ds(0, 1)], 14)
        got(part4_in.at[pl.ds(0, NR - 1), pl.ds(0, 1)], 15)
        gone(part_in.at[pl.ds(0, NC - 1), pl.ds(0, 1)], 14)
        gone(part4_in.at[pl.ds(0, NR - 1), pl.ds(0, 1)], 15)
        parts = jnp.sum(part_in[:, :1, :], axis=0) + jnp.sum(part4_in[:, :1, :], axis=0)
        tot[...] += spread(2.0 * (y + parts), tall_t[...], wide_t[...])

        def t_send(o):
            rows, lanes = o.chunk
            send(tot.at[rows, lanes], t_in.at[me], 17, o.where)

        everyone(t_send)
        t_in[me] = tot[my_rows, my_lanes]
        rr = rr_buf[...]

        @pl.when(it < ITERS - 1)
        def _():
            got(t_in.at[pl.ds(0, ND - 1)], 17)
            t_red[...] = jnp.sum(t_in[...], axis=0)
            everyone(lambda o: send(t_red, full.at[my_rows, my_lanes], 18, o.where))
            full[my_rows, my_lanes] = t_red[...]
            gone(t_in.at[pl.ds(0, ND - 1)], 17)
            got(t_in.at[pl.ds(0, ND - 1)], 18)
            gone(t_in.at[pl.ds(0, ND - 1)], 18)

            direction = vec[...]
            applied = direction + full[...]
            step = rr / jnp.broadcast_to(jnp.sum(direction * applied, keepdims=True), (8, 128))
            res = ret[...] - step[:1, :1] * applied
            ret[...] = res
            new = jnp.broadcast_to(jnp.sum(res * res, keepdims=True), (8, 128))
            beta = new / rr
            vec[...] = res + beta[:1, :1] * direction
            rr_buf[...] = new
            spread_c()
            start_k()
            out[0] += step * dir_own[...]
            out[1] -= step * (dir_own[...] + t_red[...])
            dir_own[...] = out[1] + beta * dir_own[...]

        @pl.when(it == ITERS - 1)
        def _():
            direction = vec[...]
            share = jnp.broadcast_to(jnp.sum(tot[...] * direction, keepdims=True), (8, 128))
            s_out[...] = share
            s_in[me] = share
            row0 = pl.ds(0, 1)
            everyone(lambda o: send(s_out.at[row0], s_in.at[me, row0], 18, o.where))
            got(t_in.at[pl.ds(0, ND - 1)], 17)
            got(s_in.at[pl.ds(0, ND - 1), row0], 18)
            whole = jnp.sum(s_in[:, :1, :], axis=0) + jnp.sum(direction * direction, keepdims=True)
            step = rr[:1] / whole
            out[0] += step * dir_own[...]
            out[1] -= step * (dir_own[...] + jnp.sum(t_in[...], axis=0))
            gone(t_in.at[pl.ds(0, ND - 1)], 17)
            gone(s_in.at[pl.ds(0, ND - 1), row0], 18)

        return carry

    lax.fori_loop(0, ITERS, iterate, 0)

    gone(p_cols.at[pl.ds(0, 3)], 0)
    gone(v_own.at[:, pl.ds(0, 384)], 1)
    gone(u_own.at[:, pl.ds(0, 31 * 128)], 2)
    gone(t_in.at[pl.ds(0, ND - 1)], 3)
    gone(p_rows.at[:, 0], 4)
    gone(p_rows.at[pl.ds(0, 3), 0, 0], 5)
    gone(p_rows.at[:, 0, pl.ds(0, 3)], 6)
    gone(vp_all.at[:, 0], 7)
    gone(vp_all.at[pl.ds(0, 3), 0, 0], 8)
    gone(vp_all.at[:, 0, pl.ds(0, 3)], 9)
    gone(up_all.at[pl.ds(0, 3)], 10)

    @pl.when(moved)
    def _():
        gone(p_cols.at[0], 19)
        gone(v_own.at[:, pl.ds(0, 128)], 20)
        gone(v_tile, 21)
        gone(own_t, 22)
        gone(u_tile, 23)
        gone(u_own.at[:, pl.ds(0, 128)], 24)


def local(
    right_side, eigen_basis, tile_left, tile_right, piece_owner, omega_main, damping,
    local_basis, local_omega, local_left, local_right, local_owner,
):
    vmem = pl.BlockSpec(memory_space=pltpu.VMEM)
    V = pltpu.VMEM
    far = pl.BlockSpec(memory_space=pl.ANY)
    scratch = [
        V((8, 256, 256), BF),
        V((8, 256, 256), F32),
        V((8, 256, 256), BF),
        V((8, 256, 256), BF),
        V((4, 96, 128), BF),
        V((4, 96, 128), BF),
        V((32, 96, 128), BF),
        V((1, 128), jnp.int32),
        V((4, 2, 4, 96, 512), BF),
        V((4, 96, 512), BF),
        V((96, 4096), BF),
        V((96, 512), BF),
        V((4, 2, 4, 128, 512), BF),
        V((4, 128, 512), BF),
        V((8, 256, 256), BF),
        V((8, 256, 256), BF),
        V((8, 256, 256), F32),
        V((8, 512, 256), BF),
        V((8, 256, 256), BF),
        V((512, 128), BF),
        V((256, 128), BF),
        V((512, 512), F32),
        V((512, 256), F32),
        V((512, 256), F32),
        V((512, 256), F32),
        V((1536, 256), BF),
        V((8, 8, 256), F32),
        V((8, 128), F32),
        V((32, 8, 128), F32),
        V((4, 8, 128), F32),
        V((32, 8, 128), F32),
        V((32, 8, 128), F32),
        V((4, 8, 128), F32),
        V((4, 8, 128), F32),
        V((192, 512), BF),
        V((512, 512), BF),
        V((128, 16, 128), BF),
        V((16, 128), BF),
        V((512, 512), BF),
        V((512, 256), F32),
        V((128, 8, 128), F32),
        V((8, 128), F32),
        V((8, 128), F32),
        V((128, 8, 128), F32),
        V((8, 128), F32),
        V((8, 128), F32),
        pltpu.SemaphoreType.DMA((25,)),
        pltpu.SemaphoreType.DMA((25,)),
        pltpu.SemaphoreType.DMA((6,)),
    ]
    out = pl.pallas_call(
        kernel,
        out_shape=jax.ShapeDtypeStruct((2, 8, 128), F32),
        in_specs=[vmem, vmem, far] + [vmem] * 5 + [far] * 4,
        out_specs=vmem,
        scratch_shapes=scratch,
        name="newton",
        compiler_params=pltpu.CompilerParams(
            collective_id=0, has_side_effects=True, vmem_limit_bytes=56 * 1024 * 1024
        ),
    )(
        right_side.reshape(8, 128),
        eigen_basis,
        tile_left.reshape(32, 96, 128),
        tile_right,
        piece_owner,
        local_owner,
        omega_main,
        damping.reshape(1, 512),
        local_basis,
        local_omega,
        local_left,
        local_right,
    )
    both = out.reshape(2, 1024)
    return both[0], both[1]


def solution(mesh):
    both = ("row", "col")
    placed = (
        P(both), P(both, None), P("row", "col"), P("row", "col"), P("row", "col"), P(), P(),
        P(both, None, None), P(both, None, None), P(both, None, None), P(both, None, None),
        P(both, None),
    )
    return jax.shard_map(
        local, mesh=mesh, in_specs=placed, out_specs=(P(both), P(both)), check_vma=False
    )
```

```python
import jax
import jax.numpy as jnp
from jax import lax
from jax.experimental import pallas as pl
from jax.experimental.pallas import tpu as pltpu
from jax.sharding import PartitionSpec as P

ITERS = 2
NR, NC = 4, 32
ND = NR * NC
MESH = pl.DeviceIdType.MESH
BF = jnp.bfloat16
F32 = jnp.float32
NN = (((1,), (0,)), ((), ()))
NT = (((1,), (1,)), ((), ()))
TN = (((0,), (0,)), ((), ()))


def dot(a, b, dims=NN):
    return lax.dot_general(a, b, dims, preferred_element_type=F32)


def pieces2(x):
    hi = x.astype(BF)
    return hi, (x - hi.astype(F32)).astype(BF)


def pieces3(x):
    hi = x.astype(BF)
    rest = x - hi.astype(F32)
    mid = rest.astype(BF)
    return hi, mid, (rest - mid.astype(F32)).astype(BF)


class Place:
    def __init__(self, x, h, z, low, core):
        self.where = (low * 2 + core, x * 8 + h * 4 + z)
        self.chunk = (
            pl.ds(pl.multiple_of(core * 256 + x * 64 + h * 32 + z * 8, 8), 8),
            pl.ds(pl.multiple_of(low * 128, 128), 128),
        )
        self.block = (
            pl.ds(pl.multiple_of(low * 256 + core * 128 + x * 32 + h * 16, 16), 16),
            pl.ds(pl.multiple_of(z * 128, 128), 128),
        )


def hots(owner):
    width = owner.shape[1]
    high = lax.shift_right_logical(owner, 7) & 511
    low = (lax.shift_right_logical(owner, 16) * 128) + (owner & 127)
    tall = jnp.where(lax.broadcasted_iota(jnp.int32, (512, width), 0) == high, 1.0, 0.0)
    wide = jnp.where(lax.broadcasted_iota(jnp.int32, (256, width), 0) == low, 1.0, 0.0)
    return tall.astype(BF), wide.astype(BF)


def fetch(d3, tall, wide):
    g = dot(d3, wide)
    g = g[:512] + g[512:1024] + g[1024:]
    return jnp.sum(g * tall.astype(F32), axis=0, keepdims=True)


def spread(values, tall, wide):
    x3 = jnp.concatenate(pieces3(wide.astype(F32) * values), axis=0)
    t = dot(tall, x3, NT)
    return t[:, :256] + t[:, 256:512] + t[:, 512:]


def kernel(
    rhs, p_own, u_in, v_raw, own_in, own_l, omega, damp, hbm_basis, hbm_omega, hbm_left, hbm_right,
    out,
    l_basis, l_omega, l_left, l_right, v_in, v_tile, u_tile, own_t,
    p_rows, p_cols, u_own, v_own, vp_all, up_all, at, bt, sym, tall_l, wide_l, tall_t, wide_t,
    quad, full, vec, ret, d3, c_l, c_me, c_col, c_row, part_out, part_in, part4_out, part4_in,
    s_buf, k_out, k_in, k_red, k_full, tot, t_in, t_red, s_out, s_in, dir_own, rr_buf,
    ssem, rsem, lsem,
):
    row = lax.axis_index("row")
    col = lax.axis_index("col")
    me = row * NC + col
    x = col // 8
    h = lax.rem(col // 4, 2)
    z = lax.rem(col, 4)
    core = lax.rem(row, 2)
    i = (row // 2) * 2 + h
    j = x * 8 + core * 4 + z
    moved = core != h
    kept = core == h

    def holder(ii, jj):
        return (
            (ii // 2) * 2 + lax.rem(jj // 4, 2),
            (jj // 8) * 8 + lax.rem(ii, 2) * 4 + lax.rem(jj, 4),
        )

    def file(r):
        return holder(lax.rem(i + r, NR), j)

    def dev(xx, zz):
        return (row, xx * 8 + h * 4 + zz)

    sibling = (row + 1 - 2 * core, col)

    def send(src, dst, k, where):
        pltpu.make_async_remote_copy(
            src, dst, ssem.at[k], rsem.at[k], device_id=where, device_id_type=MESH
        ).start()

    def got(ref, k):
        pltpu.make_async_copy(ref, ref, rsem.at[k]).wait()

    def gone(ref, k):
        pltpu.make_async_copy(ref, ref, ssem.at[k]).wait()

    ahead = (2, 3, 1, 0)
    y = h * 2 + row // 2
    zs = [lax.rem(z + k, 4) for k in ahead]
    ys = [lax.rem(y + k, 4) for k in ahead]
    ys = [(lax.rem(k, 2), k // 2) for k in ys]

    def far(k):
        return lax.rem(x + 2 + (k * (k + 1)) // 2, 4)

    def spots(count, inner, body):
        def step(k, carry):
            for at_inner in inner:
                body(k, *at_inner)
            return carry

        lax.fori_loop(0, count - 1, step, 0)
        for at_inner in inner[:-1]:
            body(count - 1, *at_inner)

    def everyone(body):
        inner = [(zz, yy) for zz in zs for yy in ys]

        def one(k, zz, yy):
            cc = lax.rem(core + 1 - k // 4, 2)
            body(Place(far(lax.rem(k, 4)), yy[1], zz, yy[0], cc))

        spots(8, inner, one)

    def plane(body):
        inner = [(cc, zz) for cc in (1 - core, core) for zz in zs]
        low = row // 2
        spots(4, inner, lambda k, cc, zz: body(far(k) * 8 + cc * 4 + zz, Place(far(k), h, zz, low, cc).where))

    loads = [
        pltpu.make_async_copy(src, dst, lsem.at[n])
        for n, (src, dst) in enumerate(
            [(hbm_basis, l_basis), (hbm_left, l_left), (hbm_right, l_right), (hbm_omega, l_omega)]
        )
    ]
    for load in loads:
        load.start()
    barrier = pltpu.get_barrier_semaphore()
    everyone(
        lambda o: pl.semaphore_signal(barrier, inc=1, device_id=o.where, device_id_type=MESH)
    )
    v_in[...] = v_raw[...].astype(F32).T.astype(BF).reshape(4, 96, 128)
    pl.semaphore_wait(barrier, ND - 1)

    lane_row = pl.ds(pl.multiple_of(row * 128, 128), 128)
    lane_col = pl.ds(pl.multiple_of(col * 128, 128), 128)

    @pl.when(moved)
    def _():
        send(p_own, p_cols.at[row], 19, holder(row, col))

    for r in range(1, NR):
        o = lax.rem(row + r, NR)
        send(p_own, p_cols.at[row], 0, holder(o, col))

    @pl.when(moved)
    def _():
        send(v_in, v_tile, 21, holder(row, col))
        send(own_in, own_t, 22, holder(row, col))

    @pl.when(kept)
    def _():
        p_cols[row] = p_own[...]
        v_tile[...] = v_in[...]
        own_t[...] = own_in[...]

    own = Place(x, h, z, row // 2, core)
    my_rows, my_lanes = own.chunk
    everyone(lambda o: send(rhs, vec.at[my_rows, my_lanes], 3, o.where))
    vec[my_rows, my_lanes] = rhs[...]

    def prepare(b, carry):
        basis = l_basis[b]
        at[b] = dot(l_left[b], basis).T.astype(BF)
        bt[b] = dot(l_right[b], basis).T.astype(BF)
        om = l_omega[b]
        sym[b] = 0.5 * (om + om.T)
        tall, wide = hots(own_l[pl.ds(b, 1), :])
        tall_l[b] = tall
        wide_l[b] = wide
        return carry

    for load in loads:
        load.wait()
    lax.fori_loop(0, 6, prepare, 0)
    t = 0.5 * omega[...] - damp[...]
    quad[...] = t + t.T

    @pl.when(moved)
    def _():
        got(p_cols.at[0], 19)

    A, B = pl.ds(0, 48), pl.ds(48, 48)
    for r in (1, 3, 2):
        send(p_cols.at[i, A], p_rows.at[x, core, z, A], 5, dev(x, lax.rem(z + r, 4)))
        send(p_cols.at[i, B], p_rows.at[x, core, z, B], 5, dev(lax.rem(x + r, 4), z))
    p_rows[x, core, z] = p_cols[i]

    got(p_cols.at[pl.ds(0, 3)], 0)

    @pl.when(moved)
    def _():
        got(v_tile, 21)
        got(own_t, 22)

    vp = dot(v_tile[...].reshape(384, 128), p_cols[...].reshape(384, 512), TN).astype(BF)
    vp_all[x, core, z] = vp
    C, D = pl.ds(0, 64), pl.ds(64, 64)
    for r in (1, 3, 2):
        send(vp_all.at[x, core, z, C], vp_all.at[x, core, z, C], 8, dev(x, lax.rem(z + r, 4)))
        send(vp_all.at[x, core, z, D], vp_all.at[x, core, z, D], 8, dev(lax.rem(x + r, 4), z))

    @pl.when(moved)
    def _():
        send(u_in, u_tile, 23, holder(row, col))

    @pl.when(kept)
    def _():
        pltpu.make_async_copy(u_in, u_tile, lsem.at[4]).start()

    got(p_rows.at[pl.ds(0, 3), 0, 0], 5)
    for r in (1, 3, 2):
        send(p_rows.at[x, core, :, A], p_rows.at[x, core, :, A], 6, dev(lax.rem(x + r, 4), z))
        send(p_rows.at[:, core, z, B], p_rows.at[:, core, z, B], 6, dev(x, lax.rem(z + r, 4)))

    tall, wide = hots(own_t[...])
    tall_t[...] = tall
    wide_t[...] = wide

    got(vp_all.at[pl.ds(0, 3), 0, 0], 8)
    for r in (1, 3, 2):
        send(vp_all.at[x, core, :, C], vp_all.at[x, core, :, C], 9, dev(lax.rem(x + r, 4), z))
        send(vp_all.at[:, core, z, D], vp_all.at[:, core, z, D], 9, dev(x, lax.rem(z + r, 4)))

    def u_send(k, hh, zz):
        xx = far(k)
        there = ((row // 2) * 2 + hh, xx * 8 + core * 4 + zz)
        send(u_in.at[xx * 8 + hh * 4 + zz], u_own.at[:, lane_col], 2, there)

    spots(4, [(hh, zz) for hh in (1 - h, h) for zz in zs], u_send)
    for r in range(1, NR):
        o = lax.rem(row + r, NR)
        send(v_in.at[o], v_own.at[:, lane_row], 1, holder(o, col))

    @pl.when(moved)
    def _():
        send(v_in.at[row], v_own.at[:, lane_row], 20, holder(row, col))
        send(u_in.at[col], u_own.at[:, lane_col], 24, holder(row, col))

    @pl.when(kept)
    def _():
        v_own[:, lane_row] = v_in[row]
        pltpu.make_async_copy(u_in.at[col], u_own.at[:, lane_col], lsem.at[5]).start()


    def spread_c():
        d3[...] = jnp.concatenate(pieces3(vec[...]), axis=0)
        c_own = jnp.broadcast_to(fetch(d3[...], tall_t[...], wide_t[...]), (8, 128))
        c_me[...] = c_own
        c_col[j] = c_own
        c_row[i] = c_own

        plane(lambda jj, where: send(c_me.at[pl.ds(0, 1)], c_col.at[j, pl.ds(0, 1)], 11, where))
        for r in range(1, NR):
            send(c_me.at[pl.ds(0, 1)], c_row.at[i, pl.ds(0, 1)], 12, file(r))

    def take(b, carry):
        c_l[b] = jnp.broadcast_to(fetch(d3[...], tall_l[b], wide_l[b]), (8, 256))
        return carry

    k_rows, k_lanes = own.block

    def start_k():
        c = jnp.broadcast_to(c_me[...][:1], (128, 128)).T
        c = jnp.concatenate([c] * 4, axis=1)
        vp = vp_all[x, core, z]
        up = up_all[i]
        sv = (vp.astype(F32) * c).astype(BF)
        su = (up.astype(F32) * c).astype(BF)
        k_out[...] = (dot(up, sv, TN) + dot(vp, su, TN)).astype(BF)

        def k_send(o):
            rows, lanes = o.block
            send(k_out.at[rows, lanes], k_in.at[me], 13, o.where)

        everyone(k_send)
        k_in[me] = k_out[k_rows, k_lanes]

    def turn_k():
        got(k_in.at[pl.ds(0, ND - 1)], 13)
        k_red[...] = jnp.sum(k_in[...].astype(F32), axis=0).astype(BF)
        everyone(lambda o: send(k_red, k_full.at[k_rows, k_lanes], 16, o.where))
        k_full[k_rows, k_lanes] = k_red[...]

    def blocks(b, carry):
        a = at[b].astype(F32)
        right = bt[b]
        hi, lo = pieces2(a * c_l[b][:1])
        half_t = dot(hi, right, NT) + dot(lo, right, NT)
        w = sym[b] * (half_t + half_t.T)
        hi, lo = pieces2(w)
        mixed = dot(hi, right) + dot(lo, right)
        values = 2.0 * jnp.sum(a * mixed, axis=0, keepdims=True)
        tot[...] += spread(values, tall_l[b], wide_l[b])
        return carry

    got(t_in.at[pl.ds(0, ND - 1)], 3)
    first = vec[...]
    ret[...] = first
    dir_own[...] = rhs[...]
    out[1] = rhs[...]
    out[0] = jnp.zeros_like(rhs)
    rr_buf[...] = jnp.broadcast_to(jnp.sum(first * first, keepdims=True), (8, 128))
    spread_c()
    lax.fori_loop(6, 8, prepare, 0)
    got(p_rows.at[:, 0, pl.ds(0, 3)], 6)
    send(p_rows.at[:, core], p_rows.at[:, core], 4, sibling)
    lax.fori_loop(0, 8, take, 0)

    @pl.when(moved)
    def _():
        got(u_tile, 23)

    @pl.when(kept)
    def _():
        pltpu.make_async_copy(u_in, u_tile, lsem.at[4]).wait()

    got(p_rows.at[:, 0], 4)

    def project(k, acc):
        u = u_tile[pl.ds(k * 8, 8)].reshape(768, 128)
        return acc + dot(u, p_rows[k].reshape(768, 512), TN)

    up = lax.fori_loop(0, 4, project, jnp.zeros((128, 512), F32)).astype(BF)
    up_all[i] = up
    for r in range(1, NR):
        send(up_all.at[i], up_all.at[i], 10, file(r))
    start_k()

    got(vp_all.at[:, 0, pl.ds(0, 3)], 9)
    send(vp_all.at[:, core], vp_all.at[:, core], 7, sibling)
    tot[...] = jnp.zeros((512, 256), F32)
    lax.fori_loop(0, 8, blocks, 0)
    turn_k()

    got(u_own.at[:, pl.ds(0, 31 * 128)], 2)
    got(v_own.at[:, pl.ds(0, 384)], 1)

    @pl.when(moved)
    def _():
        got(v_own.at[:, pl.ds(0, 128)], 20)
        got(u_own.at[:, pl.ds(0, 128)], 24)

    @pl.when(kept)
    def _():
        pltpu.make_async_copy(u_in.at[col], u_own.at[:, lane_col], lsem.at[5]).wait()

    got(vp_all.at[:, 0], 7)
    got(up_all.at[pl.ds(0, 3)], 10)

    def iterate(it, carry):
        got(c_col.at[pl.ds(0, NC - 1), pl.ds(0, 1)], 11)
        got(c_row.at[pl.ds(0, NR - 1), pl.ds(0, 1)], 12)
        gone(c_col.at[pl.ds(0, NC - 1), pl.ds(0, 1)], 11)
        gone(c_row.at[pl.ds(0, NR - 1), pl.ds(0, 1)], 12)

        def add_rows(k, acc):
            lanes = pl.ds(pl.multiple_of(k * 1024, 1024), 1024)
            c = c_col[pl.ds(k * 8, 8)]
            c = jnp.concatenate([c[n, :1] for n in range(8)], axis=0).T
            v = vp_all[k].reshape(8, 128, 512)
            sv = [(v[n].astype(F32) * c[:, n : n + 1]).astype(BF) for n in range(8)]
            return acc + dot(u_own[:, lanes], jnp.concatenate(sv, axis=0))

        c = c_row[...]
        c = jnp.concatenate([c[n, :1] for n in range(NR)] * 2, axis=0).T
        su = [(up_all[n].astype(F32) * c[:, n : n + 1]).astype(BF) for n in range(NR)]
        s = lax.fori_loop(0, 4, add_rows, dot(v_own[...], jnp.concatenate(su, axis=0)))
        s = s.astype(BF)

        s_buf[...] = jnp.concatenate(pieces2(s.astype(F32) * damp[...]), axis=0)

        def field(k, carry):
            lanes = pl.ds(pl.multiple_of(k * 1024, 1024), 1024)
            t = dot(s_buf[...], vp_all[k].reshape(1024, 512), NT)
            t = (t[:96] + t[96:]) * u_own[:, lanes].astype(F32)
            t = jnp.sum(t, axis=0, keepdims=True)
            for n in range(8):
                part_out[k * 8 + n] = jnp.broadcast_to(t[:, n * 128 : (n + 1) * 128], (8, 128))
            return carry

        lax.fori_loop(0, 4, field, 0)
        t = dot(s_buf[...], up_all[...].reshape(512, 512), NT)
        t = jnp.sum((t[:96] + t[96:]) * v_own[...].astype(F32), axis=0, keepdims=True)
        for n in range(NR):
            part4_out[n] = jnp.broadcast_to(t[:, n * 128 : (n + 1) * 128], (8, 128))

        plane(
            lambda jj, where: send(
                part_out.at[jj, pl.ds(0, 1)], part_in.at[j, pl.ds(0, 1)], 14, where
            )
        )
        for r in range(1, NR):
            o = lax.rem(i + r, NR)
            send(part4_out.at[o, pl.ds(0, 1)], part4_in.at[i, pl.ds(0, 1)], 15, file(r))
        part_in[j] = part_out[j]
        part4_in[i] = part4_out[i]

        @pl.when(it > 0)
        def _():
            turn_k()
            tot[...] = jnp.zeros((512, 256), F32)
            lax.fori_loop(0, 8, blocks, 0)

        got(k_in.at[pl.ds(0, ND - 1)], 16)
        gone(k_in.at[pl.ds(0, ND - 1)], 13)
        gone(k_in.at[pl.ds(0, ND - 1)], 16)
        hi, lo = pieces2(k_full[...].astype(F32) * quad[...])
        y = dot(vp_all[x, core, z], hi) + dot(vp_all[x, core, z], lo)
        y = y * up_all[i].astype(F32)
        y = y[:, :128] + y[:, 128:256] + y[:, 256:384] + y[:, 384:]
        y = jnp.sum(y.T, axis=0, keepdims=True)
        got(part_in.at[pl.ds(0, NC - 1), pl.ds(0, 1)], 14)
        got(part4_in.at[pl.ds(0, NR - 1), pl.ds(0, 1)], 15)
        gone(part_in.at[pl.ds(0, NC - 1), pl.ds(0, 1)], 14)
        gone(part4_in.at[pl.ds(0, NR - 1), pl.ds(0, 1)], 15)
        parts = jnp.sum(part_in[:, :1, :], axis=0) + jnp.sum(part4_in[:, :1, :], axis=0)
        tot[...] += spread(2.0 * (y + parts), tall_t[...], wide_t[...])

        def t_send(o):
            rows, lanes = o.chunk
            send(tot.at[rows, lanes], t_in.at[me], 17, o.where)

        everyone(t_send)
        t_in[me] = tot[my_rows, my_lanes]
        rr = rr_buf[...]

        @pl.when(it < ITERS - 1)
        def _():
            got(t_in.at[pl.ds(0, ND - 1)], 17)
            t_red[...] = jnp.sum(t_in[...], axis=0)
            everyone(lambda o: send(t_red, full.at[my_rows, my_lanes], 18, o.where))
            full[my_rows, my_lanes] = t_red[...]
            gone(t_in.at[pl.ds(0, ND - 1)], 17)
            got(t_in.at[pl.ds(0, ND - 1)], 18)
            gone(t_in.at[pl.ds(0, ND - 1)], 18)

            direction = vec[...]
            applied = direction + full[...]
            step = rr / jnp.broadcast_to(jnp.sum(direction * applied, keepdims=True), (8, 128))
            res = ret[...] - step[:1, :1] * applied
            ret[...] = res
            new = jnp.broadcast_to(jnp.sum(res * res, keepdims=True), (8, 128))
            beta = new / rr
            vec[...] = res + beta[:1, :1] * direction
            rr_buf[...] = new
            spread_c()
            start_k()
            out[0] += step * dir_own[...]
            out[1] -= step * (dir_own[...] + t_red[...])
            dir_own[...] = out[1] + beta * dir_own[...]
            lax.fori_loop(0, 8, take, 0)

        @pl.when(it == ITERS - 1)
        def _():
            direction = vec[...]
            share = jnp.broadcast_to(jnp.sum(tot[...] * direction, keepdims=True), (8, 128))
            s_out[...] = share
            s_in[me] = share
            row0 = pl.ds(0, 1)
            everyone(lambda o: send(s_out.at[row0], s_in.at[me, row0], 18, o.where))
            got(t_in.at[pl.ds(0, ND - 1)], 17)
            got(s_in.at[pl.ds(0, ND - 1), row0], 18)
            whole = jnp.sum(s_in[:, :1, :], axis=0) + jnp.sum(direction * direction, keepdims=True)
            step = rr[:1] / whole
            out[0] += step * dir_own[...]
            out[1] -= step * (dir_own[...] + jnp.sum(t_in[...], axis=0))
            gone(t_in.at[pl.ds(0, ND - 1)], 17)
            gone(s_in.at[pl.ds(0, ND - 1), row0], 18)

        return carry

    lax.fori_loop(0, ITERS, iterate, 0)

    gone(p_cols.at[pl.ds(0, 3)], 0)
    gone(v_own.at[:, pl.ds(0, 384)], 1)
    gone(u_own.at[:, pl.ds(0, 31 * 128)], 2)
    gone(t_in.at[pl.ds(0, ND - 1)], 3)
    gone(p_rows.at[:, 0], 4)
    gone(p_rows.at[pl.ds(0, 3), 0, 0], 5)
    gone(p_rows.at[:, 0, pl.ds(0, 3)], 6)
    gone(vp_all.at[:, 0], 7)
    gone(vp_all.at[pl.ds(0, 3), 0, 0], 8)
    gone(vp_all.at[:, 0, pl.ds(0, 3)], 9)
    gone(up_all.at[pl.ds(0, 3)], 10)

    @pl.when(moved)
    def _():
        gone(p_cols.at[0], 19)
        gone(v_own.at[:, pl.ds(0, 128)], 20)
        gone(v_tile, 21)
        gone(own_t, 22)
        gone(u_tile, 23)
        gone(u_own.at[:, pl.ds(0, 128)], 24)


def local(
    right_side, eigen_basis, tile_left, tile_right, piece_owner, omega_main, damping,
    local_basis, local_omega, local_left, local_right, local_owner,
):
    vmem = pl.BlockSpec(memory_space=pltpu.VMEM)
    V = pltpu.VMEM
    far = pl.BlockSpec(memory_space=pl.ANY)
    scratch = [
        V((8, 256, 256), BF),
        V((8, 256, 256), F32),
        V((8, 256, 256), BF),
        V((8, 256, 256), BF),
        V((4, 96, 128), BF),
        V((4, 96, 128), BF),
        V((32, 96, 128), BF),
        V((1, 128), jnp.int32),
        V((4, 2, 4, 96, 512), BF),
        V((4, 96, 512), BF),
        V((96, 4096), BF),
        V((96, 512), BF),
        V((4, 2, 4, 128, 512), BF),
        V((4, 128, 512), BF),
        V((8, 256, 256), BF),
        V((8, 256, 256), BF),
        V((8, 256, 256), F32),
        V((8, 512, 256), BF),
        V((8, 256, 256), BF),
        V((512, 128), BF),
        V((256, 128), BF),
        V((512, 512), F32),
        V((512, 256), F32),
        V((512, 256), F32),
        V((512, 256), F32),
        V((1536, 256), BF),
        V((8, 8, 256), F32),
        V((8, 128), F32),
        V((32, 8, 128), F32),
        V((4, 8, 128), F32),
        V((32, 8, 128), F32),
        V((32, 8, 128), F32),
        V((4, 8, 128), F32),
        V((4, 8, 128), F32),
        V((192, 512), BF),
        V((512, 512), BF),
        V((128, 16, 128), BF),
        V((16, 128), BF),
        V((512, 512), BF),
        V((512, 256), F32),
        V((128, 8, 128), F32),
        V((8, 128), F32),
        V((8, 128), F32),
        V((128, 8, 128), F32),
        V((8, 128), F32),
        V((8, 128), F32),
        pltpu.SemaphoreType.DMA((25,)),
        pltpu.SemaphoreType.DMA((25,)),
        pltpu.SemaphoreType.DMA((6,)),
    ]
    out = pl.pallas_call(
        kernel,
        out_shape=jax.ShapeDtypeStruct((2, 8, 128), F32),
        in_specs=[vmem, vmem, far] + [vmem] * 5 + [far] * 4,
        out_specs=vmem,
        scratch_shapes=scratch,
        name="newton",
        compiler_params=pltpu.CompilerParams(
            collective_id=0, has_side_effects=True, vmem_limit_bytes=56 * 1024 * 1024
        ),
    )(
        right_side.reshape(8, 128),
        eigen_basis,
        tile_left.reshape(32, 96, 128),
        tile_right,
        piece_owner,
        local_owner,
        omega_main,
        damping.reshape(1, 512),
        local_basis,
        local_omega,
        local_left,
        local_right,
    )
    both = out.reshape(2, 1024)
    return both[0], both[1]


def solution(mesh):
    both = ("row", "col")
    placed = (
        P(both), P(both, None), P("row", "col"), P("row", "col"), P("row", "col"), P(), P(),
        P(both, None, None), P(both, None, None), P(both, None, None), P(both, None, None),
        P(both, None),
    )
    return jax.shard_map(
        local, mesh=mesh, in_specs=placed, out_specs=(P(both), P(both)), check_vma=False
    )
```
